256 devices in a mesh: ctx: 32 (over x, y, core), head: 8 (over z).
Axes of the slice: x: 4, y: 4, z: 8, core: 2. Of those that a mesh axis runs over, the one named last changes fastest.
Arguments:
- q_latent: bfloat16 [4096, 36864], P('ctx', 'head'), may hold values from -4 to 4
- kv_latent: bfloat16 [4096, 576], P('ctx'), may hold values from -3 to 3
- out_grad: bfloat16 [4096, 32768], P('ctx', 'head'), may hold values from -48 to 48
- saved_out: bfloat16 [4096, 32768], P('ctx', 'head'), may hold values from -3 to 3
- group_order: int32 [64], replicated, may hold values from 0 to 63, as said below
Outputs:
- q_grad: bfloat16 [4096, 36864], P('ctx', 'head')
- kv_grad: float32 [4096, 576], P(('ctx', 'head'))
The draws below stay inside these ranges and needn't reach their ends.
Inputs may be any that keep to these rules, and one draw needn't show every extreme that they name: `group_order`: stored group slots 2 i and 2 i + 1 hold sequence groups c and 63 - c with c < 32; every group appears once.
All inputs are finite; a program needn't handle non-finite values.
Results may differ from the reference program's by a relative error of at most 0.0049.
Values may be sent and summed in bfloat16 or wider, within the bound.
No kernel may reach another device: no remote copies, remote signals or barrier semaphores. Data moves between devices by JAX's collectives and lax.ppermute only.
A program may use at most 128 MiB of HBM per device.

```python
import jax
import jax.numpy as jnp
from jax import lax

LATENT = 512
ROPE = 64
HEADS = 64
GROUP = 64
GROUPS = 64
TOKENS = 4096


def draw_q_latent(key, part):
    key = jax.random.fold_in(key, 3)
    values = jnp.clip(jax.random.normal(key, (TOKENS, HEADS, LATENT + ROPE), jnp.float32), -4.0, 4.0)
    return values.reshape(TOKENS, HEADS * (LATENT + ROPE)).astype(jnp.bfloat16)


def draw_kv_latent(key, part):
    key = jax.random.fold_in(key, 5)
    values = jnp.clip(jax.random.normal(key, (TOKENS, LATENT + ROPE), jnp.float32), -3.0, 3.0)
    return values.astype(jnp.bfloat16)


def draw_group_order(key, part):
    key = jax.random.fold_in(key, 7)
    lower = jax.random.permutation(key, GROUPS // 2).astype(jnp.int32)
    upper = GROUPS - 1 - lower
    return jnp.stack([lower, upper], axis=1).reshape(GROUPS).astype(jnp.int32)


def levels(own_key, extent, shards, least, high):
    loudness, own = 1.0, jax.random.fold_in(own_key, 6)
    for axis_at, parts in shards:
        steps = jnp.exp(jax.random.uniform(jax.random.fold_in(own, axis_at), (parts,), jnp.float32, least / len(shards), high / len(shards)))
        loudness = loudness * jnp.repeat(steps, extent[axis_at] // parts).reshape([-1 if axis == axis_at else 1 for axis in range(len(extent))])
    return loudness


def gaussian(key, dims, width, bound, cuts=(), kind=jnp.bfloat16):
    result = jax.random.normal(key, dims, jnp.float32) * width
    if len(cuts) > 0:
        result = levels(key, dims, cuts, -0.22, 0.18) * result
    return jnp.clip(result, min=-bound, max=bound).astype(kind)


def setup_inputs(seed: int = 0) -> dict:
    seeds = jax.random.split(jax.random.key(seed), 6)
    q_latent = draw_q_latent(jax.random.fold_in(seeds[5], 71), 0)
    kv_latent = draw_kv_latent(jax.random.fold_in(seeds[5], 71), 0)
    out_grad = gaussian(seeds[2], (TOKENS, HEADS * LATENT), 8.0, 48.0, ((0, 32), (1, 8)))
    saved_out = gaussian(seeds[3], (TOKENS, HEADS * LATENT), 0.5, 3.0, ((0, 32), (1, 8)))
    group_order = draw_group_order(jax.random.fold_in(seeds[5], 71), 0)
    return dict(q_latent=q_latent, kv_latent=kv_latent, out_grad=out_grad, saved_out=saved_out, group_order=group_order)


score_scale = 192.0 ** -0.5


def reference(q_latent, kv_latent, out_grad, saved_out, group_order):
    row_width = LATENT + ROPE
    row_ids = jnp.arange(TOKENS, dtype=jnp.int32)
    row_positions = group_order[row_ids // GROUP].astype(jnp.int32) * GROUP + row_ids % GROUP
    visible = row_positions[None, :] <= row_positions[:, None]
    queries = q_latent.reshape(TOKENS, HEADS, row_width).transpose(1, 0, 2)
    cotangents = out_grad.reshape(TOKENS, HEADS, LATENT).transpose(1, 0, 2)
    outputs = saved_out.reshape(TOKENS, HEADS, LATENT).transpose(1, 0, 2)
    values = kv_latent[:, :LATENT]

    def per_head(carried, inputs):
        head_query, cotangent, saved = inputs
        scores = jnp.dot(head_query, kv_latent.T, preferred_element_type=jnp.float32) * score_scale
        scores = jnp.where(visible, scores, -1e30)
        running_max = jnp.max(scores, axis=1, keepdims=True)
        log_norm = running_max + jnp.log(jnp.sum(jnp.where(visible, jnp.exp(scores - running_max), 0.0), axis=1, keepdims=True))
        weights = jnp.where(visible, jnp.exp(scores - log_norm), 0.0)
        weights_low = weights.astype(jnp.bfloat16)
        deltas = jnp.sum(cotangent.astype(jnp.float32) * saved.astype(jnp.float32), axis=1, keepdims=True)
        dweights = jnp.dot(cotangent, values.T, preferred_element_type=jnp.float32)
        dscores = (weights * (dweights - deltas) * score_scale).astype(jnp.bfloat16)
        head_grad = jnp.dot(dscores, kv_latent, preferred_element_type=jnp.float32).astype(jnp.bfloat16)
        key_term = jnp.dot(dscores.T, head_query, preferred_element_type=jnp.float32)
        value_term = jnp.dot(weights_low.T, cotangent, preferred_element_type=jnp.float32)
        carried = carried + key_term + jnp.pad(value_term, ((0, 0), (0, ROPE)))
        return carried, head_grad

    start_grad = jnp.zeros((TOKENS, row_width), jnp.float32)
    kv_grad, head_grads = lax.scan(per_head, start_grad, (queries, cotangents, outputs))
    q_grad = head_grads.transpose(1, 0, 2).reshape(TOKENS, HEADS * row_width)
    return q_grad, kv_grad
```

```python
import functools
import math

import jax
import jax.numpy as jnp
from jax import lax
from jax.experimental import pallas as pl
from jax.experimental.pallas import tpu as pltpu
from jax.sharding import Mesh, PartitionSpec as P

LATENT = 512
ROPE = 64
WIDTH = LATENT + ROPE
GROUP = 64
BLOCK = 256
PAIR = 2 * GROUP

score_scale = 192.0 ** (-0.5)
log2_scale = score_scale * math.log2(math.e)
neg_fill = -1e30

NT = (((1,), (1,)), ((), ()))


def mm(a, b):
    return jnp.dot(a, b, preferred_element_type=jnp.float32)


def twice(a):
    return jnp.concatenate([a, a], axis=1)


def grad_kernel(
    order, place, q_rows, q_cols, g_rows, g_cols, deltas, *rest, pieces, piece_y, sides, rows
):
    piece_refs = rest[:pieces]
    dq_out, keep_out, send_out = rest[pieces : pieces + 3]
    stage, keys, scores, top, total, dq_acc, dk_acc, slot_of, sem = rest[pieces + 3 :]
    pairs = stage.shape[0]
    groups = 2 * pairs
    blocks = groups * GROUP // BLOCK
    items = blocks + 1
    per_block = BLOCK // GROUP
    my_x, my_y, my_c = place[0], place[1], place[2]
    rank = (my_x * sides + my_y) * 2 + my_c

    copies = []
    for at, ref in enumerate(piece_refs):
        step_x, step_c = at // 2, at % 2
        for step_y in range(piece_y):
            at_x = lax.rem(my_x + step_x, sides)
            at_y = lax.rem(my_y + step_y, sides)
            at_c = lax.rem(my_c + step_c, 2)
            pair = (at_x * sides + at_y) * 2 + at_c
            copy = pltpu.make_async_copy(
                ref.at[step_y], stage.at[pair], sem.at[at * piece_y + step_y]
            )
            copy.start()
            copies.append(copy)

    def note(p, carry):
        slot_of[order[2 * p]] = p
        return carry

    lax.fori_loop(0, pairs, note, 0)
    top[...] = jnp.full(top.shape, neg_fill, jnp.float32)
    total[...] = jnp.zeros(total.shape, jnp.float32)
    dq_acc[...] = jnp.zeros(dq_acc.shape, jnp.float32)
    for copy in copies:
        copy.wait()

    def place_low(i, carry):
        first = stage[slot_of[2 * i]]
        second = stage[slot_of[2 * i + 1]]
        at = pl.multiple_of(i * PAIR, PAIR)
        keys[:, pl.ds(at, PAIR)] = jnp.concatenate([first[:, :GROUP], second[:, :GROUP]], axis=1)
        return carry

    def place_high(i, carry):
        first = stage[slot_of[groups - 1 - 2 * i]]
        second = stage[slot_of[groups - 2 - 2 * i]]
        at = pl.multiple_of(i * PAIR, PAIR)
        keys[:, pl.ds(at, PAIR)] = jnp.concatenate([first[:, GROUP:], second[:, GROUP:]], axis=1)
        return carry

    lax.fori_loop(0, pairs // 2, place_low, 0)
    lax.fori_loop(pairs // 2, pairs, place_high, 0)

    low_group = order[2 * rank]
    high_group = order[2 * rank + 1]
    high_blocks = lax.div(high_group, per_block) + 1

    def item(i):
        is_low = (i >= high_blocks).astype(jnp.int32)
        block = i - is_low * high_blocks
        row0 = pl.multiple_of((1 - is_low) * rows, rows)
        key0 = pl.multiple_of(block * BLOCK, BLOCK)
        return is_low, block, row0, key0

    def score_step(i, carry):
        is_low, block, row0, key0 = item(i)
        group = jnp.where(is_low == 1, low_group, high_group)
        raw = mm(q_rows[pl.ds(row0, rows), :], keys[:, pl.ds(key0, BLOCK)]) * log2_scale
        token = lax.broadcasted_iota(jnp.int32, (rows, BLOCK), 0) % GROUP
        lane = lax.broadcasted_iota(jnp.int32, (rows, BLOCK), 1)
        visible = lane - token <= group * GROUP - block * BLOCK
        t = jnp.where(visible, raw, neg_fill)
        scores[i] = t
        left, right = t[:, : BLOCK // 2], t[:, BLOCK // 2 :]
        old_top = top[pl.ds(row0, rows), :]
        new_top = jnp.maximum(old_top, jnp.maximum(left, right))
        added = jnp.exp2(left - new_top) + jnp.exp2(right - new_top)
        total[pl.ds(row0, rows), :] = total[pl.ds(row0, rows), :] * jnp.exp2(old_top - new_top) + added
        top[pl.ds(row0, rows), :] = new_top
        return carry

    lax.fori_loop(0, items, score_step, 0)

    lane_top = top[...]
    row_top = jnp.max(lane_top, axis=1, keepdims=True)
    row_sum = jnp.sum(total[...] * jnp.exp2(lane_top - row_top), axis=1, keepdims=True)
    top[...] = jnp.broadcast_to(row_top + jnp.log2(row_sum), top.shape)

    def clear(b, carry):
        at = pl.multiple_of(b * BLOCK, BLOCK)
        dk_acc[:, pl.ds(at, BLOCK)] = jnp.zeros((WIDTH, BLOCK), jnp.float32)
        return carry

    lax.fori_loop(high_blocks, blocks, clear, 0)

    def grad_step(i, carry):
        is_low, block, row0, key0 = item(i)
        key_tile = keys[:, pl.ds(key0, BLOCK)]
        weights = jnp.exp2(scores[i] - twice(top[pl.ds(row0, rows), :]))
        dweights = mm(g_rows[pl.ds(row0, rows), :], key_tile[:LATENT])
        dscores = weights * (dweights - twice(deltas[pl.ds(row0, rows), :])) * score_scale
        low = dscores.astype(jnp.bfloat16)
        weights_low = weights.astype(jnp.bfloat16)
        dq_acc[pl.ds(row0, rows), :] += lax.dot_general(
            low, key_tile, NT, preferred_element_type=jnp.float32
        )
        from_scores = mm(q_cols[:, pl.ds(row0, rows)], low)
        from_values = mm(g_cols[:, pl.ds(row0, rows)], weights_low)
        old = dk_acc[:, pl.ds(key0, BLOCK)]
        old = jnp.where(is_low == 1, old, 0.0)
        dk_acc[:LATENT, pl.ds(key0, BLOCK)] = old[:LATENT] + from_scores[:LATENT] + from_values
        dk_acc[LATENT:, pl.ds(key0, BLOCK)] = old[LATENT:] + from_scores[LATENT:]
        return carry

    lax.fori_loop(0, items, grad_step, 0)

    dq_out[...] = dq_acc[...].astype(jnp.bfloat16)

    def emit(p, carry):
        group = order[2 * p]
        low_at = pl.multiple_of(lax.div(group, 2) * PAIR, PAIR)
        high_at = pl.multiple_of(lax.div(groups - 1 - group, 2) * PAIR, PAIR)
        low_tile = dk_acc[:, pl.ds(low_at, PAIR)]
        high_tile = dk_acc[:, pl.ds(high_at, PAIR)]
        odd = lax.rem(group, 2) == 1
        mine = lax.rem(p, 2) == my_c

        def put(tile):
            tile = tile.astype(jnp.bfloat16)

            @pl.when(mine)
            def _():
                keep_out[lax.div(p, 2)] = tile

            @pl.when(jnp.logical_not(mine))
            def _():
                send_out[lax.div(p, 2)] = tile

        @pl.when(odd)
        def _():
            put(jnp.concatenate([low_tile[:, GROUP:], high_tile[:, :GROUP]], axis=1))

        @pl.when(jnp.logical_not(odd))
        def _():
            lane = lax.broadcasted_iota(jnp.int32, (WIDTH, PAIR), 1)
            put(jnp.where(lane < GROUP, low_tile, high_tile))

        return carry

    lax.fori_loop(0, pairs, emit, 0)


def run_grads(order, place, q_rows, q_cols, g_rows, g_cols, deltas, pieces, sides):
    rows = q_rows.shape[0] // 2
    piece_y = pieces[0].shape[0]
    pairs = len(pieces) * piece_y
    items = pairs * PAIR // BLOCK + 1
    vmem = pl.BlockSpec(memory_space=pltpu.VMEM)
    smem = pl.BlockSpec(memory_space=pltpu.SMEM)
    half = pairs // 2
    return pl.pallas_call(
        functools.partial(
            grad_kernel, pieces=len(pieces), piece_y=piece_y, sides=sides, rows=rows
        ),
        out_shape=(
            jax.ShapeDtypeStruct((2 * rows, WIDTH), jnp.bfloat16),
            jax.ShapeDtypeStruct((half, WIDTH, PAIR), jnp.bfloat16),
            jax.ShapeDtypeStruct((half, WIDTH, PAIR), jnp.bfloat16),
        ),
        in_specs=[smem, smem] + [vmem] * 5 + [pl.BlockSpec(memory_space=pl.ANY)] * len(pieces),
        out_specs=(vmem, vmem, vmem),
        scratch_shapes=[
            pltpu.VMEM((pairs, WIDTH, PAIR), jnp.bfloat16),
            pltpu.VMEM((WIDTH, pairs * PAIR), jnp.bfloat16),
            pltpu.VMEM((items, rows, BLOCK), jnp.float32),
            pltpu.VMEM((2 * rows, 128), jnp.float32),
            pltpu.VMEM((2 * rows, 128), jnp.float32),
            pltpu.VMEM((2 * rows, WIDTH), jnp.float32),
            pltpu.VMEM((WIDTH, pairs * PAIR), jnp.float32),
            pltpu.SMEM((2 * pairs,), jnp.int32),
            pltpu.SemaphoreType.DMA((pairs,)),
        ],
        compiler_params=pltpu.CompilerParams(vmem_limit_bytes=60 * 1024 * 1024),
        cost_estimate=pl.CostEstimate(
            flops=items * rows * BLOCK * 2 * 2752, bytes_accessed=24 << 20, transcendentals=0
        ),
        name="latent_grads",
    )(order, place, q_rows, q_cols, g_rows, g_cols, deltas, *pieces)


def shift(a, axis, size, step):
    return lax.ppermute(a, axis, [(i, (i - step) % size) for i in range(size)])


def head_rows(a, width):
    tokens = a.shape[0]
    heads = a.shape[1] // width
    a = a.reshape(2, tokens // 2, heads, width).transpose(0, 2, 1, 3)
    return a.reshape(tokens * heads, width)


def shards(q_latent, kv_latent, out_grad, saved_out, group_order, *, sides, depth):
    tokens = q_latent.shape[0]
    heads = q_latent.shape[1] // WIDTH
    place = jnp.stack([lax.axis_index("x"), lax.axis_index("y"), lax.axis_index("c")]).astype(jnp.int32)

    own = kv_latent.T
    along_y = jnp.stack([own] + [shift(own, "y", sides, d) for d in range(1, sides)])
    along_x = [along_y] + [shift(along_y, "x", sides, d) for d in range(1, sides)]
    pieces = []
    for piece in along_x:
        pieces += [piece, shift(piece, "c", 2, 1)]

    q_rows = head_rows(q_latent, WIDTH)
    g_rows = head_rows(out_grad, LATENT)
    delta = jnp.sum(
        (out_grad.astype(jnp.float32) * saved_out.astype(jnp.float32)).reshape(
            2, tokens // 2, heads, LATENT
        ),
        axis=3,
    )
    delta = delta.transpose(0, 2, 1).reshape(tokens * heads, 1)
    deltas = jnp.broadcast_to(delta, (tokens * heads, 128))

    dq, keep, send = run_grads(
        group_order, place, q_rows, q_rows.T, g_rows, g_rows.T, deltas, pieces, sides
    )
    q_grad = dq.reshape(2, heads, tokens // 2, WIDTH).transpose(0, 2, 1, 3)
    q_grad = q_grad.reshape(tokens, heads * WIDTH)

    def added(parts):
        return jnp.sum(parts.astype(jnp.float32), axis=0)

    received = lax.ppermute(send, "c", [(0, 1), (1, 0)])
    both = (keep.astype(jnp.float32) + received.astype(jnp.float32)).astype(jnp.bfloat16)
    parts = lax.all_to_all(both, ("x", "y"), 0, 0, tiled=True)
    summed = added(parts)
    by_head = summed.reshape(WIDTH, depth, PAIR // depth).transpose(1, 2, 0)
    parts = lax.all_to_all(by_head.astype(jnp.bfloat16), "z", 0, 0, tiled=True)
    return q_grad, added(parts)


def solution(mesh):
    ctx, depth = mesh.shape["ctx"], mesh.shape["head"]
    sides = math.isqrt(ctx // 2)
    finer = Mesh(mesh.devices.reshape(sides, sides, 2, depth), ("x", "y", "c", "z"))
    ctx_axes = ("x", "y", "c")
    placed = (P(ctx_axes, "z"), P(ctx_axes, None), P(ctx_axes, "z"), P(ctx_axes, "z"), P())
    return jax.shard_map(
        functools.partial(shards, sides=sides, depth=depth),
        mesh=finer,
        in_specs=placed,
        out_specs=(P(ctx_axes, "z"), P(("x", "y", "c", "z"), None)),
        check_vma=False,
    )
```

```python
import functools
import math

import jax
import jax.numpy as jnp
from jax import lax
from jax.experimental import pallas as pl
from jax.experimental.pallas import tpu as pltpu
from jax.sharding import Mesh, PartitionSpec as P

LATENT = 512
ROPE = 64
WIDTH = LATENT + ROPE
HALF = WIDTH // 2
GROUP = 64
BLOCK = 256
PAIR = 2 * GROUP

score_scale = 192.0 ** (-0.5)
log2_scale = score_scale * math.log2(math.e)
neg_fill = -1e30

NT = (((1,), (1,)), ((), ()))


def mm(a, b):
    return jnp.dot(a, b, preferred_element_type=jnp.float32)


def twice(a):
    return jnp.concatenate([a, a], axis=1)


def grad_kernel(
    order, place, q_rows, q_cols, g_rows, g_cols, deltas, *rest, sides, rows
):
    pieces = 4 * sides
    piece_refs = rest[:pieces]
    dq_out, keep_a, keep_b, send_a, send_b = rest[pieces : pieces + 5]
    stage, keys, scores, top, total, dq_acc, dk_acc, slot_of, sem = rest[pieces + 5 :]
    pairs = stage.shape[0]
    groups = 2 * pairs
    blocks = groups * GROUP // BLOCK
    items = blocks + 1
    per_block = BLOCK // GROUP
    my_x, my_y, my_c = place[0], place[1], place[2]
    rank = (my_x * sides + my_y) * 2 + my_c

    copies = []
    for at, ref in enumerate(piece_refs):
        part, rest_at = at // (2 * sides), at % (2 * sides)
        first, step_c = rest_at // 2, rest_at % 2
        for second in range(sides):
            step_x, step_y = (first, second) if part == 0 else (second, first)
            at_x = lax.rem(my_x + step_x, sides)
            at_y = lax.rem(my_y + step_y, sides)
            at_c = lax.rem(my_c + step_c, 2)
            pair = (at_x * sides + at_y) * 2 + at_c
            copy = pltpu.make_async_copy(
                ref.at[second],
                stage.at[pair, pl.ds(part * HALF, HALF)],
                sem.at[at * sides + second],
            )
            copy.start()
            copies.append(copy)

    def note(p, carry):
        slot_of[order[2 * p]] = p
        return carry

    lax.fori_loop(0, pairs, note, 0)
    top[...] = jnp.full(top.shape, neg_fill, jnp.float32)
    total[...] = jnp.zeros(total.shape, jnp.float32)
    dq_acc[...] = jnp.zeros(dq_acc.shape, jnp.float32)
    for copy in copies:
        copy.wait()

    def place_low(i, carry):
        first = stage[slot_of[2 * i]]
        second = stage[slot_of[2 * i + 1]]
        at = pl.multiple_of(i * PAIR, PAIR)
        keys[:, pl.ds(at, PAIR)] = jnp.concatenate([first[:, :GROUP], second[:, :GROUP]], axis=1)
        return carry

    def place_high(i, carry):
        first = stage[slot_of[groups - 1 - 2 * i]]
        second = stage[slot_of[groups - 2 - 2 * i]]
        at = pl.multiple_of(i * PAIR, PAIR)
        keys[:, pl.ds(at, PAIR)] = jnp.concatenate([first[:, GROUP:], second[:, GROUP:]], axis=1)
        return carry

    lax.fori_loop(0, pairs // 2, place_low, 0)
    lax.fori_loop(pairs // 2, pairs, place_high, 0)

    low_group = order[2 * rank]
    high_group = order[2 * rank + 1]
    high_blocks = lax.div(high_group, per_block) + 1

    def item(i):
        is_low = (i >= high_blocks).astype(jnp.int32)
        block = i - is_low * high_blocks
        row0 = pl.multiple_of((1 - is_low) * rows, rows)
        key0 = pl.multiple_of(block * BLOCK, BLOCK)
        return is_low, block, row0, key0

    def score_step(i, carry):
        is_low, block, row0, key0 = item(i)
        group = jnp.where(is_low == 1, low_group, high_group)
        raw = mm(q_rows[pl.ds(row0, rows), :], keys[:, pl.ds(key0, BLOCK)]) * log2_scale
        token = lax.broadcasted_iota(jnp.int32, (rows, BLOCK), 0) % GROUP
        lane = lax.broadcasted_iota(jnp.int32, (rows, BLOCK), 1)
        visible = lane - token <= group * GROUP - block * BLOCK
        t = jnp.where(visible, raw, neg_fill)
        scores[i] = t
        left, right = t[:, : BLOCK // 2], t[:, BLOCK // 2 :]
        old_top = top[pl.ds(row0, rows), :]
        new_top = jnp.maximum(old_top, jnp.maximum(left, right))
        added = jnp.exp2(left - new_top) + jnp.exp2(right - new_top)
        total[pl.ds(row0, rows), :] = total[pl.ds(row0, rows), :] * jnp.exp2(old_top - new_top) + added
        top[pl.ds(row0, rows), :] = new_top
        return carry

    lax.fori_loop(0, items, score_step, 0)

    lane_top = top[...]
    row_top = jnp.max(lane_top, axis=1, keepdims=True)
    row_sum = jnp.sum(total[...] * jnp.exp2(lane_top - row_top), axis=1, keepdims=True)
    top[...] = jnp.broadcast_to(row_top + jnp.log2(row_sum), top.shape)

    def clear(b, carry):
        at = pl.multiple_of(b * BLOCK, BLOCK)
        dk_acc[:, pl.ds(at, BLOCK)] = jnp.zeros((WIDTH, BLOCK), jnp.float32)
        return carry

    lax.fori_loop(high_blocks, blocks, clear, 0)

    def grad_step(i, carry):
        is_low, block, row0, key0 = item(i)
        key_tile = keys[:, pl.ds(key0, BLOCK)]
        weights = jnp.exp2(scores[i] - twice(top[pl.ds(row0, rows), :]))
        dweights = mm(g_rows[pl.ds(row0, rows), :], key_tile[:LATENT])
        dscores = weights * (dweights - twice(deltas[pl.ds(row0, rows), :])) * score_scale
        low = dscores.astype(jnp.bfloat16)
        weights_low = weights.astype(jnp.bfloat16)
        dq_acc[pl.ds(row0, rows), :] += lax.dot_general(
            low, key_tile, NT, preferred_element_type=jnp.float32
        )
        from_scores = mm(q_cols[:, pl.ds(row0, rows)], low)
        from_values = mm(g_cols[:, pl.ds(row0, rows)], weights_low)
        old = dk_acc[:, pl.ds(key0, BLOCK)]
        old = jnp.where(is_low == 1, old, 0.0)
        dk_acc[:LATENT, pl.ds(key0, BLOCK)] = old[:LATENT] + from_scores[:LATENT] + from_values
        dk_acc[LATENT:, pl.ds(key0, BLOCK)] = old[LATENT:] + from_scores[LATENT:]
        return carry

    lax.fori_loop(0, items, grad_step, 0)

    dq_out[...] = dq_acc[...].astype(jnp.bfloat16)

    def emit(p, carry):
        group = order[2 * p]
        low_at = pl.multiple_of(lax.div(group, 2) * PAIR, PAIR)
        high_at = pl.multiple_of(lax.div(groups - 1 - group, 2) * PAIR, PAIR)
        low_tile = dk_acc[:, pl.ds(low_at, PAIR)]
        high_tile = dk_acc[:, pl.ds(high_at, PAIR)]
        odd = lax.rem(group, 2) == 1
        mine = lax.rem(p, 2) == my_c
        step_x = lax.rem(lax.div(p, 2 * sides) - my_x + sides, sides)
        step_y = lax.rem(lax.rem(lax.div(p, 2), sides) - my_y + sides, sides)

        def put(tile):
            tile = tile.astype(jnp.bfloat16)

            @pl.when(mine)
            def _():
                keep_a[step_x, step_y] = tile[:HALF]
                keep_b[step_y, step_x] = tile[HALF:]

            @pl.when(jnp.logical_not(mine))
            def _():
                send_a[step_x, step_y] = tile[:HALF]
                send_b[step_y, step_x] = tile[HALF:]

        @pl.when(odd)
        def _():
            put(jnp.concatenate([low_tile[:, GROUP:], high_tile[:, :GROUP]], axis=1))

        @pl.when(jnp.logical_not(odd))
        def _():
            lane = lax.broadcasted_iota(jnp.int32, (WIDTH, PAIR), 1)
            put(jnp.where(lane < GROUP, low_tile, high_tile))

        return carry

    lax.fori_loop(0, pairs, emit, 0)


def run_grads(order, place, q_rows, q_cols, g_rows, g_cols, deltas, pieces, sides):
    rows = q_rows.shape[0] // 2
    pairs = 2 * sides * sides
    items = pairs * PAIR // BLOCK + 1
    vmem = pl.BlockSpec(memory_space=pltpu.VMEM)
    smem = pl.BlockSpec(memory_space=pltpu.SMEM)
    part = jax.ShapeDtypeStruct((sides, sides, HALF, PAIR), jnp.bfloat16)
    return pl.pallas_call(
        functools.partial(grad_kernel, sides=sides, rows=rows),
        out_shape=(jax.ShapeDtypeStruct((2 * rows, WIDTH), jnp.bfloat16), part, part, part, part),
        in_specs=[smem, smem] + [vmem] * 5 + [pl.BlockSpec(memory_space=pl.ANY)] * len(pieces),
        out_specs=(vmem,) * 5,
        scratch_shapes=[
            pltpu.VMEM((pairs, WIDTH, PAIR), jnp.bfloat16),
            pltpu.VMEM((WIDTH, pairs * PAIR), jnp.bfloat16),
            pltpu.VMEM((items, rows, BLOCK), jnp.float32),
            pltpu.VMEM((2 * rows, 128), jnp.float32),
            pltpu.VMEM((2 * rows, 128), jnp.float32),
            pltpu.VMEM((2 * rows, WIDTH), jnp.float32),
            pltpu.VMEM((WIDTH, pairs * PAIR), jnp.float32),
            pltpu.SMEM((2 * pairs,), jnp.int32),
            pltpu.SemaphoreType.DMA((2 * pairs,)),
        ],
        compiler_params=pltpu.CompilerParams(vmem_limit_bytes=60 * 1024 * 1024),
        cost_estimate=pl.CostEstimate(
            flops=items * rows * BLOCK * 2 * 2752, bytes_accessed=24 << 20, transcendentals=0
        ),
        name="latent_grads",
    )(order, place, q_rows, q_cols, g_rows, g_cols, deltas, *pieces)


def shift(a, axis, size, step):
    return lax.ppermute(a, axis, [(i, (i - step) % size) for i in range(size)])


def head_rows(a, width):
    tokens = a.shape[0]
    heads = a.shape[1] // width
    a = a.reshape(2, tokens // 2, heads, width).transpose(0, 2, 1, 3)
    return a.reshape(tokens * heads, width)


def shards(q_latent, kv_latent, out_grad, saved_out, group_order, *, sides, depth):
    tokens = q_latent.shape[0]
    heads = q_latent.shape[1] // WIDTH
    place = jnp.stack([lax.axis_index("x"), lax.axis_index("y"), lax.axis_index("c")]).astype(jnp.int32)

    def spread(a, axis):
        return [a] + [shift(a, axis, sides, d) for d in range(1, sides)]

    own = kv_latent.T
    part_a = spread(jnp.stack(spread(own[:HALF], "y")), "x")
    part_b = spread(jnp.stack(spread(own[HALF:], "x")), "y")

    q_rows = head_rows(q_latent, WIDTH)
    g_rows = head_rows(out_grad, LATENT)
    delta = jnp.sum(
        (out_grad.astype(jnp.float32) * saved_out.astype(jnp.float32)).reshape(
            2, tokens // 2, heads, LATENT
        ),
        axis=3,
    )
    delta = delta.transpose(0, 2, 1).reshape(tokens * heads, 1)
    deltas = jnp.broadcast_to(delta, (tokens * heads, 128))
    local = (q_rows, q_rows.T, g_rows, g_rows.T, deltas)
    arrived, local = lax.optimization_barrier((part_a[1:] + part_b[1:], local))
    pieces = []
    for piece in [part_a[0]] + arrived[: sides - 1] + [part_b[0]] + arrived[sides - 1 :]:
        pieces += [piece, shift(piece, "c", 2, 1)]

    dq, keep_a, keep_b, send_a, send_b = run_grads(group_order, place, *local, pieces, sides)
    q_grad = dq.reshape(2, heads, tokens // 2, WIDTH).transpose(0, 2, 1, 3)
    q_grad = q_grad.reshape(tokens, heads * WIDTH)

    def reduce_to_owner(keep, send, axes):
        received = shift(send, "c", 2, 1)
        total = keep.astype(jnp.float32) + received.astype(jnp.float32)
        for axis in axes:
            low = total.astype(jnp.bfloat16)
            moved = [shift(low[d], axis, sides, -d) for d in range(1, sides)]
            total = total[0]
            for part in moved:
                total = total + part.astype(jnp.float32)
        return total

    summed = jnp.concatenate(
        [reduce_to_owner(keep_a, send_a, ("x", "y")), reduce_to_owner(keep_b, send_b, ("y", "x"))]
    )
    by_head = summed.reshape(WIDTH, depth, PAIR // depth).transpose(1, 2, 0)
    parts = lax.all_to_all(by_head.astype(jnp.bfloat16), "z", 0, 0, tiled=True)
    return q_grad, jnp.sum(parts.astype(jnp.float32), axis=0)


def solution(mesh):
    ctx, depth = mesh.shape["ctx"], mesh.shape["head"]
    sides = math.isqrt(ctx // 2)
    finer = Mesh(mesh.devices.reshape(sides, sides, 2, depth), ("x", "y", "c", "z"))
    ctx_axes = ("x", "y", "c")
    placed = (P(ctx_axes, "z"), P(ctx_axes, None), P(ctx_axes, "z"), P(ctx_axes, "z"), P())
    return jax.shard_map(
        functools.partial(shards, sides=sides, depth=depth),
        mesh=finer,
        in_specs=placed,
        out_specs=(P(ctx_axes, "z"), P(("x", "y", "c", "z"), None)),
        check_vma=False,
    )
```

```python
import functools
import math

import jax
import jax.numpy as jnp
from jax import lax
from jax.experimental import pallas as pl
from jax.experimental.pallas import tpu as pltpu
from jax.sharding import Mesh, PartitionSpec as P

LATENT = 512
ROPE = 64
WIDTH = LATENT + ROPE
HALF = WIDTH // 2
GROUP = 64
BLOCK = 256
PAIR = 2 * GROUP

score_scale = 192.0 ** (-0.5)
log2_scale = score_scale * math.log2(math.e)
neg_fill = -1e30

NT = (((1,), (1,)), ((), ()))


def mm(a, b):
    return jnp.dot(a, b, preferred_element_type=jnp.float32)


def twice(a):
    return jnp.concatenate([a, a], axis=1)


def on_chip(a):
    return pltpu.with_memory_space_constraint(a, pltpu.VMEM)


def visit(items, step, pair_step):
    step(0)

    def body(j, carry):
        pair_step(2 * j + 1, 2 * j + 2)
        return carry

    lax.fori_loop(0, (items - 1) // 2, body, 0)


def key_sums(order, place, q_cols, g_cols, dscores, weights, tiles, fetch, *, sides, rows):
    width, latents = q_cols.shape[0], g_cols.shape[0]
    groups = 4 * sides * sides
    blocks = groups * GROUP // BLOCK
    rank = (place[0] * sides + place[1]) * 2 + place[2]
    high_blocks = lax.div(order[2 * rank + 1], BLOCK // GROUP) + 1
    low_blocks = blocks + 1 - high_blocks

    def term(i, half):
        if fetch is not None:
            fetch(i)
        at = half * rows
        from_scores = mm(q_cols[:, at : at + rows], dscores[i])
        from_values = mm(g_cols[:, at : at + rows], weights[i])
        if latents == width:
            return [from_scores + from_values]
        return [from_scores[:latents] + from_values, from_scores[latents:]]

    def put(b, parts):
        at = pl.multiple_of(b * BLOCK, BLOCK)
        row = 0
        for part in parts:
            tiles[row : row + part.shape[0], pl.ds(at, BLOCK)] = part.astype(jnp.bfloat16)
            row += part.shape[0]

    def both(b, carry):
        high = term(b, 1)
        low = term(high_blocks + b, 0)
        put(b, [h + l for h, l in zip(high, low)])
        return carry

    def two(j, carry):
        b = low_blocks + 1 + 2 * j
        first = term(b, 1)
        second = term(b + 1, 1)
        put(b, first)
        put(b + 1, second)
        return carry

    def clear(b, carry):
        at = pl.multiple_of(b * BLOCK, BLOCK)
        tiles[:, pl.ds(at, BLOCK)] = jnp.zeros((width, BLOCK), jnp.bfloat16)
        return carry

    lax.fori_loop(0, low_blocks, both, 0)
    put(low_blocks, term(low_blocks, 1))
    lax.fori_loop(0, lax.div(high_blocks - low_blocks - 1, 2), two, 0)
    lax.fori_loop(high_blocks, blocks, clear, 0)


def emit_tiles(order, place, tiles, keep, send, *, sides, swap):
    groups = 4 * sides * sides
    my_x, my_y, my_c = place[0], place[1], place[2]

    def owner(p, ref, at):
        group = order[2 * p]
        low_at = pl.multiple_of(lax.div(group, 2) * PAIR, PAIR)
        high_at = pl.multiple_of(lax.div(groups - 1 - group, 2) * PAIR, PAIR)
        low = tiles[:, pl.ds(low_at, PAIR)]
        high = tiles[:, pl.ds(high_at, PAIR)]
        odd = lax.rem(group, 2) == 1

        @pl.when(odd)
        def _():
            ref[at[0], at[1]] = jnp.concatenate([low[:, GROUP:], high[:, :GROUP]], axis=1)

        @pl.when(jnp.logical_not(odd))
        def _():
            ref[at[0], at[1]] = jnp.concatenate([low[:, :GROUP], high[:, GROUP:]], axis=1)

    def chip(i, carry):
        step_x = lax.rem(lax.div(i, sides) - my_x + sides, sides)
        step_y = lax.rem(lax.rem(i, sides) - my_y + sides, sides)
        at = (step_y, step_x) if swap else (step_x, step_y)
        owner(2 * i + 1 - my_c, send, at)
        owner(2 * i + my_c, keep, at)
        return carry

    lax.fori_loop(0, sides * sides, chip, 0)


def weights_kernel(order, place, q_in, g_in, q_cols_in, g_cols_in, deltas_in, *rest, sides, rows):
    pieces = 4 * sides
    piece_refs = rest[:pieces]
    keys, weights, dscores, keep, send = rest[pieces : pieces + 5]
    (
        stage, scores, dweights, top, total, q_rows, g_rows, q_cols, g_cols, deltas, tiles,
        slot_of, sem, own_sem,
    ) = rest[pieces + 5 :]
    pairs = stage.shape[0]
    groups = 2 * pairs
    blocks = groups * GROUP // BLOCK
    items = blocks + 1
    my_x, my_y, my_c = place[0], place[1], place[2]
    rank = (my_x * sides + my_y) * 2 + my_c

    copies = []
    for at, ref in enumerate(piece_refs):
        part, rest_at = at // (2 * sides), at % (2 * sides)
        first, step_c = rest_at // 2, rest_at % 2
        for second in range(sides):
            step_x, step_y = (first, second) if part == 0 else (second, first)
            at_x = lax.rem(my_x + step_x, sides)
            at_y = lax.rem(my_y + step_y, sides)
            at_c = lax.rem(my_c + step_c, 2)
            pair = (at_x * sides + at_y) * 2 + at_c
            copy = pltpu.make_async_copy(
                ref.at[second],
                stage.at[pair, pl.ds(part * HALF, HALF)],
                sem.at[at * sides + second],
            )
            copy.start()
            copies.append(copy)
    own = [
        pltpu.make_async_copy(src, dst, own_sem.at[at])
        for at, (src, dst) in enumerate(
            [
                (q_in, q_rows),
                (g_in, g_rows),
                (deltas_in, deltas),
                (q_cols_in.at[pl.ds(0, HALF)], q_cols),
                (g_cols_in.at[pl.ds(0, HALF)], g_cols),
            ]
        )
    ]
    for copy in own:
        copy.start()

    def note(p, carry):
        slot_of[order[2 * p]] = p
        return carry

    lax.fori_loop(0, pairs, note, 0)
    top[...] = jnp.full(top.shape, neg_fill, jnp.float32)
    total[...] = jnp.zeros(total.shape, jnp.float32)
    for copy in copies:
        copy.wait()

    def place_low(j, carry):
        for i in (2 * j, 2 * j + 1):
            first = stage[slot_of[2 * i]]
            second = stage[slot_of[2 * i + 1]]
            at = pl.multiple_of(i * PAIR, PAIR)
            keys[:, pl.ds(at, PAIR)] = jnp.concatenate([first[:, :GROUP], second[:, :GROUP]], axis=1)
        return carry

    def place_high(j, carry):
        for i in (2 * j, 2 * j + 1):
            first = stage[slot_of[groups - 1 - 2 * i]]
            second = stage[slot_of[groups - 2 - 2 * i]]
            at = pl.multiple_of(i * PAIR, PAIR)
            keys[:, pl.ds(at, PAIR)] = jnp.concatenate([first[:, GROUP:], second[:, GROUP:]], axis=1)
        return carry

    lax.fori_loop(0, pairs // 4, place_low, 0)
    lax.fori_loop(pairs // 4, pairs // 2, place_high, 0)
    for copy in own:
        copy.wait()

    low_group = order[2 * rank]
    high_group = order[2 * rank + 1]
    high_blocks = lax.div(high_group, BLOCK // GROUP) + 1

    def score_step(i):
        is_low = (i >= high_blocks).astype(jnp.int32)
        block = i - is_low * high_blocks
        row0 = pl.multiple_of((1 - is_low) * rows, rows)
        key0 = pl.multiple_of(block * BLOCK, BLOCK)
        group = jnp.where(is_low == 1, low_group, high_group)
        key_tile = keys[:, pl.ds(key0, BLOCK)]
        raw = mm(q_rows[pl.ds(row0, rows), :], key_tile) * log2_scale
        dweights[i] = mm(g_rows[pl.ds(row0, rows), :], key_tile[:LATENT])
        token = lax.broadcasted_iota(jnp.int32, (rows, BLOCK), 0) % GROUP
        lane = lax.broadcasted_iota(jnp.int32, (rows, BLOCK), 1)
        visible = lane - token <= group * GROUP - block * BLOCK
        t = jnp.where(visible, raw, neg_fill)
        scores[i] = t
        left, right = t[:, : BLOCK // 2], t[:, BLOCK // 2 :]
        old_top = top[pl.ds(row0, rows), :]
        new_top = jnp.maximum(old_top, jnp.maximum(left, right))
        added = jnp.exp2(left - new_top) + jnp.exp2(right - new_top)
        total[pl.ds(row0, rows), :] = total[pl.ds(row0, rows), :] * jnp.exp2(old_top - new_top) + added
        top[pl.ds(row0, rows), :] = new_top

    def score_pair(i, j):
        score_step(i)
        score_step(j)

    visit(items, score_step, score_pair)

    lane_top = top[...]
    row_top = jnp.max(lane_top, axis=1, keepdims=True)
    row_sum = jnp.sum(total[...] * jnp.exp2(lane_top - row_top), axis=1, keepdims=True)
    top[...] = jnp.broadcast_to(row_top + jnp.log2(row_sum), top.shape)

    def weigh(i):
        row0 = pl.multiple_of((i < high_blocks).astype(jnp.int32) * rows, rows)
        w = jnp.exp2(scores[i] - twice(top[pl.ds(row0, rows), :]))
        ds = w * (dweights[i] - twice(deltas[pl.ds(row0, rows), :])) * score_scale
        weights[i] = w.astype(jnp.bfloat16)
        dscores[i] = ds.astype(jnp.bfloat16)

    key_sums(
        order, place, q_cols, g_cols, dscores, weights, tiles, weigh, sides=sides, rows=rows
    )
    emit_tiles(order, place, tiles, keep, send, sides=sides, swap=False)


def keys_kernel(
    order, place, q_cols_in, g_cols_in, weights, dscores, keep, send, q_cols, g_cols, tiles,
    own_sem, *, sides, rows,
):
    own = [
        pltpu.make_async_copy(q_cols_in.at[pl.ds(HALF, HALF)], q_cols, own_sem.at[0]),
        pltpu.make_async_copy(g_cols_in.at[pl.ds(HALF, LATENT - HALF)], g_cols, own_sem.at[1]),
    ]
    for copy in own:
        copy.start()

    for copy in own:
        copy.wait()

    key_sums(
        order, place, q_cols, g_cols, dscores, weights, tiles, None, sides=sides, rows=rows
    )
    emit_tiles(order, place, tiles, keep, send, sides=sides, swap=True)


def query_kernel(order, place, dscores, keys, out, acc, *, sides, rows):
    items = dscores.shape[0]
    rank = (place[0] * sides + place[1]) * 2 + place[2]
    high_blocks = lax.div(order[2 * rank + 1], BLOCK // GROUP) + 1
    acc[...] = jnp.zeros(acc.shape, jnp.float32)

    def step(i):
        is_low = (i >= high_blocks).astype(jnp.int32)
        row0 = pl.multiple_of((1 - is_low) * rows, rows)
        key0 = pl.multiple_of((i - is_low * high_blocks) * BLOCK, BLOCK)
        acc[pl.ds(row0, rows), :] += lax.dot_general(
            dscores[i], keys[:, pl.ds(key0, BLOCK)], NT, preferred_element_type=jnp.float32
        )

    def pair_step(i, j):
        step(i)
        step(j)

    visit(items, step, pair_step)
    out[...] = acc[...].astype(jnp.bfloat16)


def run_weights(order, place, local, pieces, sides):
    rows = local[0].shape[0] // 2
    pairs = 2 * sides * sides
    items = pairs * PAIR // BLOCK + 1
    vmem = pl.BlockSpec(memory_space=pltpu.VMEM)
    smem = pl.BlockSpec(memory_space=pltpu.SMEM)
    hbm = pl.BlockSpec(memory_space=pl.ANY)
    bf16, f32 = jnp.bfloat16, jnp.float32
    part = jax.ShapeDtypeStruct((sides, sides, HALF, PAIR), bf16)
    block = pltpu.VMEM((items, rows, BLOCK), bf16)
    return pl.pallas_call(
        functools.partial(weights_kernel, sides=sides, rows=rows),
        out_shape=(pltpu.VMEM((WIDTH, pairs * PAIR), bf16), block, block, part, part),
        in_specs=[smem, smem] + [hbm] * (5 + len(pieces)),
        out_specs=(vmem,) * 5,
        scratch_shapes=[
            pltpu.VMEM((pairs, WIDTH, PAIR), bf16),
            pltpu.VMEM((items, rows, BLOCK), f32),
            pltpu.VMEM((items, rows, BLOCK), f32),
            pltpu.VMEM((2 * rows, 128), f32),
            pltpu.VMEM((2 * rows, 128), f32),
            pltpu.VMEM((2 * rows, WIDTH), bf16),
            pltpu.VMEM((2 * rows, LATENT), bf16),
            pltpu.VMEM((HALF, 2 * rows), bf16),
            pltpu.VMEM((HALF, 2 * rows), bf16),
            pltpu.VMEM((2 * rows, 128), f32),
            pltpu.VMEM((HALF, pairs * PAIR), bf16),
            pltpu.SMEM((2 * pairs,), jnp.int32),
            pltpu.SemaphoreType.DMA((2 * pairs,)),
            pltpu.SemaphoreType.DMA((5,)),
        ],
        compiler_params=pltpu.CompilerParams(vmem_limit_bytes=40 * 1024 * 1024),
        cost_estimate=pl.CostEstimate(
            flops=items * rows * BLOCK * 2 * 1664, bytes_accessed=24 << 20, transcendentals=0
        ),
        name="latent_weights",
    )(order, place, *local, *pieces)


def run_keys(order, place, q_cols, g_cols, weights, dscores, sides):
    items, rows = weights.shape[:2]
    pairs = 2 * sides * sides
    vmem = pl.BlockSpec(memory_space=pltpu.VMEM)
    smem = pl.BlockSpec(memory_space=pltpu.SMEM)
    hbm = pl.BlockSpec(memory_space=pl.ANY)
    bf16 = jnp.bfloat16
    part = jax.ShapeDtypeStruct((sides, sides, HALF, PAIR), bf16)
    return pl.pallas_call(
        functools.partial(keys_kernel, sides=sides, rows=rows),
        out_shape=(part, part),
        in_specs=[smem, smem, hbm, hbm, vmem, vmem],
        out_specs=(vmem, vmem),
        scratch_shapes=[
            pltpu.VMEM((HALF, 2 * rows), bf16),
            pltpu.VMEM((LATENT - HALF, 2 * rows), bf16),
            pltpu.VMEM((HALF, pairs * PAIR), bf16),
            pltpu.SemaphoreType.DMA((2,)),
        ],
        compiler_params=pltpu.CompilerParams(vmem_limit_bytes=24 * 1024 * 1024),
        cost_estimate=pl.CostEstimate(
            flops=items * rows * BLOCK * 2 * 512, bytes_accessed=12 << 20, transcendentals=0
        ),
        name="latent_keys",
    )(order, place, q_cols, g_cols, on_chip(weights), on_chip(dscores))


def run_queries(order, place, dscores, keys, sides):
    items, rows = dscores.shape[:2]
    vmem = pl.BlockSpec(memory_space=pltpu.VMEM)
    smem = pl.BlockSpec(memory_space=pltpu.SMEM)
    hbm = pl.BlockSpec(memory_space=pl.ANY)
    return pl.pallas_call(
        functools.partial(query_kernel, sides=sides, rows=rows),
        out_shape=jax.ShapeDtypeStruct((2 * rows, WIDTH), jnp.bfloat16),
        in_specs=[smem, smem, vmem, vmem],
        out_specs=vmem,
        scratch_shapes=[pltpu.VMEM((2 * rows, WIDTH), jnp.float32)],
        compiler_params=pltpu.CompilerParams(vmem_limit_bytes=24 * 1024 * 1024),
        cost_estimate=pl.CostEstimate(
            flops=items * rows * BLOCK * 2 * WIDTH, bytes_accessed=10 << 20, transcendentals=0
        ),
        name="latent_queries",
    )(order, place, on_chip(dscores), on_chip(keys))


def shift(a, axis, size, step):
    return lax.ppermute(a, axis, [(i, (i - step) % size) for i in range(size)])


def head_rows(a, width):
    tokens = a.shape[0]
    heads = a.shape[1] // width
    a = a.reshape(2, tokens // 2, heads, width).transpose(0, 2, 1, 3)
    return a.reshape(tokens * heads, width)


def shards(q_latent, kv_latent, out_grad, saved_out, group_order, *, sides, depth):
    tokens = q_latent.shape[0]
    heads = q_latent.shape[1] // WIDTH
    place = jnp.stack([lax.axis_index("x"), lax.axis_index("y"), lax.axis_index("c")]).astype(jnp.int32)

    def spread(a, axis):
        return [a] + [shift(a, axis, sides, d) for d in range(1, sides)]

    own = kv_latent.T
    part_a = spread(jnp.stack(spread(own[:HALF], "y")), "x")
    part_b = spread(jnp.stack(spread(own[HALF:], "x")), "y")

    q_rows = head_rows(q_latent, WIDTH)
    g_rows = head_rows(out_grad, LATENT)
    delta = jnp.sum(
        (out_grad.astype(jnp.float32) * saved_out.astype(jnp.float32)).reshape(
            2, tokens // 2, heads, LATENT
        ),
        axis=3,
    )
    delta = delta.transpose(0, 2, 1).reshape(tokens * heads, 1)
    deltas = jnp.broadcast_to(delta, (tokens * heads, 128))
    local = (q_rows, g_rows, q_rows.T, g_rows.T, deltas)
    arrived, local = lax.optimization_barrier((part_a[1:] + part_b[1:], local))
    pieces = []
    for piece in [part_a[0]] + arrived[: sides - 1] + [part_b[0]] + arrived[sides - 1 :]:
        pieces += [piece, shift(piece, "c", 2, 1)]

    keys, weights, dscores, keep_a, send_a = run_weights(group_order, place, local, pieces, sides)
    got_a = shift(send_a, "c", 2, 1)
    keep_b, send_b = run_keys(group_order, place, local[2], local[3], weights, dscores, sides)
    got_b = shift(send_b, "c", 2, 1)

    def first_sum(keep, got):
        total = keep.astype(jnp.float32) + got.astype(jnp.float32)
        return total[0], [total[d].astype(jnp.bfloat16) for d in range(1, sides)]

    def exchange(axis, total, low):
        for d in range(1, sides):
            total = total + shift(low[d - 1], axis, sides, -d).astype(jnp.float32)
        return total

    total_a, low_a = first_sum(keep_a, got_a)
    total_b, low_b = first_sum(keep_b, got_b)
    low_b, dscores = lax.optimization_barrier((low_b, dscores))
    dq = run_queries(group_order, place, dscores, keys, sides)
    q_grad = dq.reshape(2, heads, tokens // 2, WIDTH).transpose(0, 2, 1, 3)
    q_grad = q_grad.reshape(tokens, heads * WIDTH)
    total_a = exchange("x", total_a, low_a)
    total_b = exchange("y", total_b, low_b)
    total_a, total_b, q_grad = lax.optimization_barrier((total_a, total_b, q_grad))

    def last(total, axis):
        low = [total[d].astype(jnp.bfloat16) for d in range(1, sides)]
        return exchange(axis, total[0], low)

    summed = jnp.concatenate([last(total_a, "y"), last(total_b, "x")])
    by_head = summed.reshape(WIDTH, depth, PAIR // depth).transpose(1, 2, 0)
    parts = lax.all_to_all(by_head.astype(jnp.bfloat16), "z", 0, 0, tiled=True)
    return q_grad, jnp.sum(parts.astype(jnp.float32), axis=0)


def solution(mesh):
    ctx, depth = mesh.shape["ctx"], mesh.shape["head"]
    sides = math.isqrt(ctx // 2)
    finer = Mesh(mesh.devices.reshape(sides, sides, 2, depth), ("x", "y", "c", "z"))
    ctx_axes = ("x", "y", "c")
    placed = (P(ctx_axes, "z"), P(ctx_axes, None), P(ctx_axes, "z"), P(ctx_axes, "z"), P())
    return jax.shard_map(
        functools.partial(shards, sides=sides, depth=depth),
        mesh=finer,
        in_specs=placed,
        out_specs=(P(ctx_axes, "z"), P(("x", "y", "c", "z"), None)),
        check_vma=False,
    )
```

```python
import functools
import math

import jax
import jax.numpy as jnp
from jax import lax
from jax.experimental import pallas as pl
from jax.experimental.pallas import tpu as pltpu
from jax.sharding import Mesh, PartitionSpec as P

LATENT = 512
ROPE = 64
WIDTH = LATENT + ROPE
HALF = WIDTH // 2
GROUP = 64
BLOCK = 256
PAIR = 2 * GROUP

score_scale = 192.0 ** (-0.5)
log2_scale = score_scale * math.log2(math.e)
neg_fill = -1e30

NT = (((1,), (1,)), ((), ()))


def mm(a, b):
    return jnp.dot(a, b, preferred_element_type=jnp.float32)


def twice(a):
    return jnp.concatenate([a, a], axis=1)


def on_chip(a):
    return pltpu.with_memory_space_constraint(a, pltpu.VMEM)


def visit(items, step, pair_step):
    step(0)

    def body(j, carry):
        pair_step(2 * j + 1, 2 * j + 2)
        return carry

    lax.fori_loop(0, (items - 1) // 2, body, 0)


def key_sums(order, place, q_cols, g_cols, tiles, weigh, *, sides, rows):
    groups = 4 * sides * sides
    blocks = groups * GROUP // BLOCK
    rank = (place[0] * sides + place[1]) * 2 + place[2]
    high_blocks = lax.div(order[2 * rank + 1], BLOCK // GROUP) + 1
    low_blocks = blocks + 1 - high_blocks

    def term(i, half):
        dscores, weights = weigh(i)
        at = half * rows
        from_scores = mm(q_cols[:, at : at + rows], dscores)
        from_values = mm(g_cols[:, at : at + rows], weights)
        return from_scores[:LATENT] + from_values, from_scores[LATENT:]

    def put(b, parts):
        at = pl.multiple_of(b * BLOCK, BLOCK)
        tiles[:LATENT, pl.ds(at, BLOCK)] = parts[0].astype(jnp.bfloat16)
        tiles[LATENT:, pl.ds(at, BLOCK)] = parts[1].astype(jnp.bfloat16)

    def both(b, carry):
        high = term(b, 1)
        low = term(high_blocks + b, 0)
        put(b, [h + l for h, l in zip(high, low)])
        return carry

    def two(j, carry):
        b = low_blocks + 1 + 2 * j
        first = term(b, 1)
        second = term(b + 1, 1)
        put(b, first)
        put(b + 1, second)
        return carry

    def clear(b, carry):
        at = pl.multiple_of(b * BLOCK, BLOCK)
        tiles[:, pl.ds(at, BLOCK)] = jnp.zeros((WIDTH, BLOCK), jnp.bfloat16)
        return carry

    lax.fori_loop(0, low_blocks, both, 0)
    put(low_blocks, term(low_blocks, 1))
    lax.fori_loop(0, lax.div(high_blocks - low_blocks - 1, 2), two, 0)
    lax.fori_loop(high_blocks, blocks, clear, 0)


def emit_tiles(order, place, tiles, keep, send, *, sides):
    groups = 4 * sides * sides
    my_x, my_y, my_c = place[0], place[1], place[2]
    lane = lax.broadcasted_iota(jnp.int32, (HALF, PAIR), 1)

    def pair(p):
        group = order[2 * p]
        odd = lax.rem(group, 2)
        low = lax.div(group, 2)
        high = lax.div(groups - 1 - group, 2)
        first = pl.multiple_of(jnp.where(odd == 1, high, low) * PAIR, PAIR)
        second = pl.multiple_of(jnp.where(odd == 1, low, high) * PAIR, PAIR)
        step_x = lax.rem(lax.div(p, 2 * sides) - my_x + sides, sides)
        step_y = lax.rem(lax.rem(lax.div(p, 2), sides) - my_y + sides, sides)
        for core, ref in ((1 - my_c, send), (my_c, keep)):
            at = pl.ds(pl.multiple_of(core * HALF, HALF), HALF)
            tile = jnp.where(
                lane < GROUP, tiles[at, pl.ds(first, PAIR)], tiles[at, pl.ds(second, PAIR)]
            )
            turned = jnp.concatenate([tile[:, GROUP:], tile[:, :GROUP]], axis=1)
            step1 = jnp.where(core == 0, step_x, step_y)
            step2 = jnp.where(core == 0, step_y, step_x)
            ref[step1, step2, lax.rem(p, 2)] = jnp.where(odd == 1, turned, tile)

    def body(j, carry):
        pair(2 * j)
        pair(2 * j + 1)
        return carry

    lax.fori_loop(0, sides * sides, body, 0)


def rows_kernel(q, g, o, q_rows, g_rows, q_cols, g_cols, deltas, mark):
    mark[...] = jnp.zeros(mark.shape, jnp.float32)
    tokens = q.shape[0] // 2
    heads = q.shape[1] // WIDTH
    for half in range(2):
        for head in range(heads):
            at = (half * heads + head) * tokens
            own = slice(half * tokens, half * tokens + tokens)
            grads = g[own, head * LATENT : (head + 1) * LATENT]
            saved = o[own, head * LATENT : (head + 1) * LATENT]
            q_rows[at : at + tokens, :] = q[own, head * WIDTH : (head + 1) * WIDTH]
            g_rows[at : at + tokens, :] = grads
            delta = jnp.sum(grads.astype(jnp.float32) * saved.astype(jnp.float32), axis=1, keepdims=True)
            deltas[at : at + tokens, :] = jnp.broadcast_to(delta, (tokens, 128))
    for at in range(0, 2 * heads * tokens, 128):
        q_cols[:, at : at + 128] = q_rows[at : at + 128, :].T
        g_cols[:, at : at + 128] = g_rows[at : at + 128, :].T


def run_rows(q, g, o):
    tokens = q.shape[0]
    rows = tokens * q.shape[1] // WIDTH
    bf16 = jnp.bfloat16
    vmem = pl.BlockSpec(memory_space=pltpu.VMEM)
    return pl.pallas_call(
        rows_kernel,
        out_shape=(
            pltpu.VMEM((rows, WIDTH), bf16),
            pltpu.VMEM((rows, LATENT), bf16),
            pltpu.VMEM((WIDTH, rows), bf16),
            pltpu.VMEM((LATENT, rows), bf16),
            pltpu.VMEM((rows, 128), jnp.float32),
            jax.ShapeDtypeStruct((8, 128), jnp.float32),
        ),
        in_specs=[vmem] * 3,
        out_specs=(vmem,) * 6,
        compiler_params=pltpu.CompilerParams(vmem_limit_bytes=32 * 1024 * 1024),
        cost_estimate=pl.CostEstimate(flops=1 << 20, bytes_accessed=24 << 20, transcendentals=0),
        name="latent_rows",
    )(q, g, o)


def grads_kernel(order, place, q_rows, g_rows, q_cols, g_cols, deltas, *rest, sides, rows):
    pieces = 2 * sides
    piece_refs = rest[:pieces]
    keys, dscores, keep, send = rest[pieces : pieces + 4]
    stage, scores, dweights, top, total, tiles, slot_of, sem = rest[pieces + 4 :]
    pairs = stage.shape[0]
    groups = 2 * pairs
    blocks = groups * GROUP // BLOCK
    items = blocks + 1
    my_x, my_y, my_c = place[0], place[1], place[2]
    rank = (my_x * sides + my_y) * 2 + my_c

    copies = []
    for at, ref in enumerate(piece_refs):
        step2 = at % sides
        holder = my_c if at < sides else 1 - my_c
        half = pl.multiple_of(holder * HALF, HALF)
        for step1 in range(sides):
            at_x = lax.rem(my_x + jnp.where(holder == 0, step2, step1), sides)
            at_y = lax.rem(my_y + jnp.where(holder == 0, step1, step2), sides)
            for step_c in range(2):
                pair = (at_x * sides + at_y) * 2 + lax.rem(holder + step_c, 2)
                copy = pltpu.make_async_copy(
                    ref.at[step1, step_c],
                    stage.at[pair, pl.ds(half, HALF)],
                    sem.at[(at * sides + step1) * 2 + step_c],
                )
                copy.start()
                copies.append(copy)

    def note(p, carry):
        slot_of[order[2 * p]] = p
        return carry

    lax.fori_loop(0, pairs, note, 0)
    top[...] = jnp.full(top.shape, neg_fill, jnp.float32)
    total[...] = jnp.zeros(total.shape, jnp.float32)
    for copy in copies:
        copy.wait()

    def place_low(j, carry):
        for i in (2 * j, 2 * j + 1):
            first = stage[slot_of[2 * i]]
            second = stage[slot_of[2 * i + 1]]
            at = pl.multiple_of(i * PAIR, PAIR)
            keys[:, pl.ds(at, PAIR)] = jnp.concatenate([first[:, :GROUP], second[:, :GROUP]], axis=1)
        return carry

    def place_high(j, carry):
        for i in (2 * j, 2 * j + 1):
            first = stage[slot_of[groups - 1 - 2 * i]]
            second = stage[slot_of[groups - 2 - 2 * i]]
            at = pl.multiple_of(i * PAIR, PAIR)
            keys[:, pl.ds(at, PAIR)] = jnp.concatenate([first[:, GROUP:], second[:, GROUP:]], axis=1)
        return carry

    lax.fori_loop(0, pairs // 4, place_low, 0)
    lax.fori_loop(pairs // 4, pairs // 2, place_high, 0)

    low_group = order[2 * rank]
    high_group = order[2 * rank + 1]
    high_blocks = lax.div(high_group, BLOCK // GROUP) + 1

    def score_step(i):
        is_low = (i >= high_blocks).astype(jnp.int32)
        block = i - is_low * high_blocks
        row0 = pl.multiple_of((1 - is_low) * rows, rows)
        key0 = pl.multiple_of(block * BLOCK, BLOCK)
        group = jnp.where(is_low == 1, low_group, high_group)
        key_tile = keys[:, pl.ds(key0, BLOCK)]
        raw = mm(q_rows[pl.ds(row0, rows), :], key_tile) * log2_scale
        dweights[i] = mm(g_rows[pl.ds(row0, rows), :], key_tile[:LATENT])
        token = lax.broadcasted_iota(jnp.int32, (rows, BLOCK), 0) % GROUP
        lane = lax.broadcasted_iota(jnp.int32, (rows, BLOCK), 1)
        visible = lane - token <= group * GROUP - block * BLOCK
        t = jnp.where(visible, raw, neg_fill)
        scores[i] = t
        left, right = t[:, : BLOCK // 2], t[:, BLOCK // 2 :]
        old_top = top[pl.ds(row0, rows), :]
        new_top = jnp.maximum(old_top, jnp.maximum(left, right))
        added = jnp.exp2(left - new_top) + jnp.exp2(right - new_top)
        total[pl.ds(row0, rows), :] = total[pl.ds(row0, rows), :] * jnp.exp2(old_top - new_top) + added
        top[pl.ds(row0, rows), :] = new_top

    def score_pair(i, j):
        score_step(i)
        score_step(j)

    visit(items, score_step, score_pair)

    lane_top = top[...]
    row_top = jnp.max(lane_top, axis=1, keepdims=True)
    row_sum = jnp.sum(total[...] * jnp.exp2(lane_top - row_top), axis=1, keepdims=True)
    top[...] = jnp.broadcast_to(row_top + jnp.log2(row_sum), top.shape)

    def weigh(i):
        row0 = pl.multiple_of((i < high_blocks).astype(jnp.int32) * rows, rows)
        w = jnp.exp2(scores[i] - twice(top[pl.ds(row0, rows), :]))
        ds = w * (dweights[i] - twice(deltas[pl.ds(row0, rows), :])) * score_scale
        ds = ds.astype(jnp.bfloat16)
        dscores[i] = ds
        return ds, w.astype(jnp.bfloat16)

    key_sums(order, place, q_cols, g_cols, tiles, weigh, sides=sides, rows=rows)
    emit_tiles(order, place, tiles, keep, send, sides=sides)


def query_kernel(order, place, dscores, keys, out, acc, *, sides, rows):
    items = dscores.shape[0]
    rank = (place[0] * sides + place[1]) * 2 + place[2]
    high_blocks = lax.div(order[2 * rank + 1], BLOCK // GROUP) + 1
    low_blocks = items - high_blocks
    acc[...] = jnp.zeros(acc.shape, jnp.float32)

    def term(i, key0):
        key0 = pl.multiple_of(key0, BLOCK)
        return lax.dot_general(
            dscores[i], keys[:, pl.ds(key0, BLOCK)], NT, preferred_element_type=jnp.float32
        )

    def high(j, carry):
        acc[rows:, :] += term(2 * j, 2 * j * BLOCK) + term(2 * j + 1, (2 * j + 1) * BLOCK)
        return carry

    def low(j, carry):
        i = high_blocks + 2 * j
        acc[:rows, :] += term(i, 2 * j * BLOCK) + term(i + 1, (2 * j + 1) * BLOCK)
        return carry

    lax.fori_loop(0, lax.div(high_blocks, 2), high, 0)
    lax.fori_loop(0, lax.div(low_blocks, 2), low, 0)
    odd_high = lax.rem(high_blocks, 2)
    row0 = pl.multiple_of(odd_high * rows, rows)
    block = jnp.where(odd_high == 1, high_blocks, low_blocks) - 1
    last = block + (1 - odd_high) * high_blocks
    acc[pl.ds(row0, rows), :] += term(last, block * BLOCK)

    tokens = out.shape[0] // 2
    heads = rows // tokens
    for half in range(2):
        for head in range(heads):
            at = (half * heads + head) * tokens
            out[half * tokens : (half + 1) * tokens, head * WIDTH : (head + 1) * WIDTH] = acc[
                at : at + tokens, :
            ].astype(jnp.bfloat16)


def run_grads(order, place, local, pieces, sides):
    rows = local[0].shape[0] // 2
    pairs = 2 * sides * sides
    items = pairs * PAIR // BLOCK + 1
    vmem = pl.BlockSpec(memory_space=pltpu.VMEM)
    smem = pl.BlockSpec(memory_space=pltpu.SMEM)
    hbm = pl.BlockSpec(memory_space=pl.ANY)
    bf16, f32 = jnp.bfloat16, jnp.float32
    part = jax.ShapeDtypeStruct((sides, sides, 2, HALF, PAIR), bf16)
    return pl.pallas_call(
        functools.partial(grads_kernel, sides=sides, rows=rows),
        out_shape=(
            pltpu.VMEM((WIDTH, pairs * PAIR), bf16),
            pltpu.VMEM((items, rows, BLOCK), bf16),
            part,
            part,
        ),
        in_specs=[smem, smem] + [vmem] * 5 + [hbm] * len(pieces),
        out_specs=(vmem,) * 4,
        scratch_shapes=[
            pltpu.VMEM((pairs, WIDTH, PAIR), bf16),
            pltpu.VMEM((items, rows, BLOCK), f32),
            pltpu.VMEM((items, rows, BLOCK), f32),
            pltpu.VMEM((2 * rows, 128), f32),
            pltpu.VMEM((2 * rows, 128), f32),
            pltpu.VMEM((WIDTH, pairs * PAIR), bf16),
            pltpu.SMEM((2 * pairs,), jnp.int32),
            pltpu.SemaphoreType.DMA((2 * pairs,)),
        ],
        compiler_params=pltpu.CompilerParams(vmem_limit_bytes=42 * 1024 * 1024),
        cost_estimate=pl.CostEstimate(
            flops=items * rows * BLOCK * 2 * 2176, bytes_accessed=24 << 20, transcendentals=0
        ),
        name="latent_grads",
    )(order, place, *[on_chip(a) for a in local], *pieces)


def run_queries(order, place, dscores, keys, sides, out_shape):
    items, rows = dscores.shape[:2]
    vmem = pl.BlockSpec(memory_space=pltpu.VMEM)
    smem = pl.BlockSpec(memory_space=pltpu.SMEM)
    return pl.pallas_call(
        functools.partial(query_kernel, sides=sides, rows=rows),
        out_shape=jax.ShapeDtypeStruct(out_shape, jnp.bfloat16),
        in_specs=[smem, smem, vmem, vmem],
        out_specs=vmem,
        scratch_shapes=[pltpu.VMEM((2 * rows, WIDTH), jnp.float32)],
        compiler_params=pltpu.CompilerParams(vmem_limit_bytes=24 * 1024 * 1024),
        cost_estimate=pl.CostEstimate(
            flops=items * rows * BLOCK * 2 * WIDTH, bytes_accessed=10 << 20, transcendentals=0
        ),
        name="latent_queries",
    )(order, place, on_chip(dscores), on_chip(keys))


def hop(a, sides, stage, step):
    moves = []
    for x in range(sides):
        for y in range(sides):
            for c in range(2):
                along_y = stage == c
                from_x = x if along_y else (x + step) % sides
                from_y = (y + step) % sides if along_y else y
                moves.append(((from_x * sides + from_y) * 2 + c, (x * sides + y) * 2 + c))
    return lax.ppermute(a, ("x", "y", "c"), moves)


def swap(a):
    return lax.ppermute(a, "c", [(0, 1), (1, 0)])


def shards(q_latent, kv_latent, out_grad, saved_out, group_order, *, sides, depth):
    my_c = lax.axis_index("c")
    place = jnp.stack([lax.axis_index("x"), lax.axis_index("y"), my_c]).astype(jnp.int32)

    own = kv_latent.T
    first, second = own[:HALF], own[HALF:]
    mine = jnp.where(my_c == 0, first, second)
    both = jnp.stack([mine, swap(jnp.where(my_c == 0, second, first))])
    line = jnp.stack([both] + [hop(both, sides, 0, d) for d in range(1, sides)])
    far = [hop(line, sides, 1, d) for d in range(1, sides)]
    *local, mark = run_rows(q_latent, out_grad, saved_out)
    far, mark = lax.optimization_barrier((far, mark))
    pieces = [line] + far
    pieces = pieces + [swap(piece) for piece in pieces]

    keys, dscores, keep, send = run_grads(group_order, place, local, pieces, sides)
    total = keep.astype(jnp.float32) + swap(send).astype(jnp.float32)
    low = [total[d].astype(jnp.bfloat16) for d in range(1, sides)]
    low, dscores = lax.optimization_barrier((low, dscores))
    q_grad = run_queries(group_order, place, dscores, keys, sides, q_latent.shape)
    total = total[0]
    for d in range(1, sides):
        total = total + hop(low[d - 1], sides, 1, -d).astype(jnp.float32)
    total, q_grad = lax.optimization_barrier((total, q_grad))
    low = [total[d].astype(jnp.bfloat16) for d in range(1, sides)]
    total = total[0]
    for d in range(1, sides):
        total = total + hop(low[d - 1], sides, 0, -d).astype(jnp.float32)

    each = PAIR // depth
    by_owner = total.reshape(2, HALF, depth, each).transpose(0, 2, 3, 1)
    by_owner = by_owner.reshape(2 * depth, each, HALF).astype(jnp.bfloat16)
    parts = lax.all_to_all(by_owner, ("c", "z"), 0, 0, tiled=True)
    parts = jnp.sum(parts.astype(jnp.float32).reshape(2, depth, each, HALF), axis=1)
    return q_grad, jnp.concatenate([parts[0], parts[1]], axis=1)


def solution(mesh):
    ctx, depth = mesh.shape["ctx"], mesh.shape["head"]
    sides = math.isqrt(ctx // 2)
    finer = Mesh(mesh.devices.reshape(sides, sides, 2, depth), ("x", "y", "c", "z"))
    ctx_axes = ("x", "y", "c")
    placed = (P(ctx_axes, "z"), P(ctx_axes, None), P(ctx_axes, "z"), P(ctx_axes, "z"), P())
    return jax.shard_map(
        functools.partial(shards, sides=sides, depth=depth),
        mesh=finer,
        in_specs=placed,
        out_specs=(P(ctx_axes, "z"), P(("x", "y", "c", "z"), None)),
        check_vma=False,
    )
```

```python
import functools
import math

import jax
import jax.numpy as jnp
from jax import lax
from jax.experimental import pallas as pl
from jax.experimental.pallas import tpu as pltpu
from jax.sharding import Mesh, PartitionSpec as P

LATENT = 512
ROPE = 64
WIDTH = LATENT + ROPE
HALF = WIDTH // 2
GROUP = 64
BLOCK = 256
PAIR = 2 * GROUP

score_scale = 192.0 ** (-0.5)
log2_scale = score_scale * math.log2(math.e)
neg_fill = -1e30

NT = (((1,), (1,)), ((), ()))


def mm(a, b):
    return jnp.dot(a, b, preferred_element_type=jnp.float32)


def twice(a):
    return jnp.concatenate([a, a], axis=1)


def on_chip(a):
    return pltpu.with_memory_space_constraint(a, pltpu.VMEM)


def here():
    return lax.axis_index("x"), lax.axis_index("y"), lax.axis_index("c")


def own_kernel(order, keys, mine, theirs, *, sides):
    my_x, my_y, my_c = here()
    odd = lax.rem(order[2 * ((my_x * sides + my_y) * 2 + my_c)], 2)
    tile = keys[...]
    turned = jnp.concatenate([tile[:, GROUP:], tile[:, :GROUP]], axis=1)
    tile = jnp.where(odd == 1, turned, tile)
    mine[...] = jnp.where(my_c == 0, tile[:HALF], tile[HALF:])
    theirs[...] = jnp.where(my_c == 0, tile[HALF:], tile[:HALF])


def run_own(order, keys, sides):
    half = jax.ShapeDtypeStruct((HALF, PAIR), jnp.bfloat16)
    vmem = pl.BlockSpec(memory_space=pltpu.VMEM)
    return pl.pallas_call(
        functools.partial(own_kernel, sides=sides),
        out_shape=(half, half),
        in_specs=[pl.BlockSpec(memory_space=pltpu.SMEM), vmem],
        out_specs=(vmem, vmem),
        name="latent_own",
    )(order, keys)


def owner_kernel(order, first, *rest, sides):
    parts, out = rest[:-1], rest[-1]
    my_x, my_y, _ = here()
    for core in range(2):
        total = first[core]
        for part in parts:
            total = total + part[core].astype(jnp.float32)
        odd = lax.rem(order[2 * ((my_x * sides + my_y) * 2 + core)], 2)
        turned = jnp.concatenate([total[:, GROUP:], total[:, :GROUP]], axis=1)
        total = jnp.where(odd == 1, turned, total)
        out[core * PAIR : (core + 1) * PAIR, :] = total.astype(jnp.bfloat16).T


def run_owner(order, first, parts, sides):
    vmem = pl.BlockSpec(memory_space=pltpu.VMEM)
    return pl.pallas_call(
        functools.partial(owner_kernel, sides=sides),
        out_shape=jax.ShapeDtypeStruct((2 * PAIR, HALF), jnp.bfloat16),
        in_specs=[pl.BlockSpec(memory_space=pltpu.SMEM)] + [vmem] * (1 + len(parts)),
        out_specs=vmem,
        name="latent_owner",
    )(order, *[on_chip(a) for a in (first, *parts)])


def key_sums(order, q_cols, g_cols, slot_of, keep, send, weigh, *, sides, rows):
    groups = 4 * sides * sides
    per_block = BLOCK // GROUP
    blocks = groups // per_block
    my_x, my_y, my_c = here()
    rank = (my_x * sides + my_y) * 2 + my_c
    high_blocks = lax.div(order[2 * rank + 1], per_block) + 1
    low_blocks = blocks + 1 - high_blocks

    def term(i, half):
        dscores, weights = weigh(i)
        at = half * rows
        return mm(q_cols[:, at : at + rows], dscores) + mm(g_cols[:, at : at + rows], weights)

    def put(b, tile):
        tile = tile.astype(jnp.bfloat16)
        for j in range(per_block):
            p = slot_of[b * per_block + j]
            step_x = lax.rem(lax.div(p, 2 * sides) - my_x + sides, sides)
            step_y = lax.rem(lax.rem(lax.div(p, 2), sides) - my_y + sides, sides)
            step1 = jnp.where(my_c == 0, step_x, step_y)
            step2 = jnp.where(my_c == 0, step_y, step_x)
            core = lax.rem(p, 2)
            lanes = pl.ds(j % 2 * GROUP, GROUP)
            keep[step1, step2, core, :, lanes] = tile[:HALF, j * GROUP : (j + 1) * GROUP]
            send[step2, step1, core, :, lanes] = tile[HALF:, j * GROUP : (j + 1) * GROUP]

    def both(b, carry):
        high = term(b, 1)
        put(b, high + term(high_blocks + b, 0))
        return carry

    def two(j, carry):
        b = low_blocks + 1 + 2 * j
        first = term(b, 1)
        second = term(b + 1, 1)
        put(b, first)
        put(b + 1, second)
        return carry

    def clear(b, carry):
        put(b, jnp.zeros((WIDTH, BLOCK), jnp.float32))
        return carry

    lax.fori_loop(0, low_blocks, both, 0)
    put(low_blocks, term(low_blocks, 1))
    lax.fori_loop(0, lax.div(high_blocks - low_blocks - 1, 2), two, 0)
    lax.fori_loop(high_blocks, blocks, clear, 0)


def spread_rows(core, q, g, o, q_rows, g_rows, q_cols, g_cols, deltas):
    tokens = q.shape[0] // 2
    heads = q.shape[1] // WIDTH
    for half in range(2):
        for head in range(heads):
            at = (half * heads + head) * tokens
            own = slice(half * tokens, half * tokens + tokens)
            grads = g[own, head * LATENT : (head + 1) * LATENT]
            saved = o[own, head * LATENT : (head + 1) * LATENT]
            q_rows[at : at + tokens, :] = q[own, head * WIDTH : (head + 1) * WIDTH]
            g_rows[at : at + tokens, :] = grads
            delta = jnp.sum(grads.astype(jnp.float32) * saved.astype(jnp.float32), axis=1, keepdims=True)
            deltas[at : at + tokens, :] = jnp.broadcast_to(delta, (tokens, 128))
    first = pl.multiple_of(core * HALF, HALF)
    second = pl.multiple_of((1 - core) * HALF, HALF)
    g_cols[pl.ds(second, HALF), :] = jnp.zeros((HALF, g_cols.shape[1]), jnp.bfloat16)
    for at in range(0, 2 * heads * tokens, 128):
        q_turned = q_rows[at : at + 128, :].T
        g_turned = g_rows[at : at + 128, :].T
        q_cols[pl.ds(first, HALF), at : at + 128] = q_turned[:HALF]
        q_cols[pl.ds(second, HALF), at : at + 128] = q_turned[HALF:]
        g_cols[pl.ds(first, HALF), at : at + 128] = g_turned[:HALF]
        g_cols[pl.ds(second, LATENT - HALF), at : at + 128] = g_turned[HALF:]


def grads_kernel(order, q_in, g_in, o_in, *rest, sides, rows):
    pieces = 2 * sides
    piece_refs = rest[:pieces]
    keys, dscores, keep, send = rest[pieces : pieces + 4]
    (
            scores, dweights, top, total, q, g, o, q_rows, g_rows, q_cols, g_cols,
        deltas, slot_of, own_sem,
    ) = rest[pieces + 4 :]
    pairs = keys.shape[1] // PAIR
    groups = 2 * pairs
    blocks = groups * GROUP // BLOCK
    items = blocks + 1
    my_x, my_y, my_c = here()
    rank = (my_x * sides + my_y) * 2 + my_c

    own = [
        pltpu.make_async_copy(src, dst, own_sem.at[at])
        for at, (src, dst) in enumerate([(q_in, q), (g_in, g), (o_in, o)])
    ]
    for copy in own:
        copy.start()
    def note(p, carry):
        slot_of[order[2 * p]] = p
        slot_of[order[2 * p + 1]] = p
        return carry

    lax.fori_loop(0, pairs, note, 0)
    top[...] = jnp.full(top.shape, neg_fill, jnp.float32)
    total[...] = jnp.zeros(total.shape, jnp.float32)

    for at, ref in enumerate(piece_refs):
        step2 = at % sides
        holder = my_c if at < sides else 1 - my_c
        half = pl.ds(pl.multiple_of(holder * HALF, HALF), HALF)
        for step1 in range(sides):
            at_x = lax.rem(my_x + jnp.where(holder == 0, step2, step1), sides)
            at_y = lax.rem(my_y + jnp.where(holder == 0, step1, step2), sides)
            for step_c in range(2):
                pair = (at_x * sides + at_y) * 2 + lax.rem(holder + step_c, 2)
                tile = ref[step1, step_c]
                turn = lax.rem(order[2 * pair], 2)
                even = lax.div(order[2 * pair + turn], 2) * PAIR
                odd = lax.div(order[2 * pair + 1 - turn], 2) * PAIR
                evens = keys.at[half, pl.ds(pl.multiple_of(even, PAIR), PAIR)]
                odds = keys.at[half, pl.ds(pl.multiple_of(odd, PAIR), PAIR)]
                evens[:, :GROUP] = tile[:, :GROUP]
                odds[:, GROUP:] = tile[:, GROUP:]
    for copy in own:
        copy.wait()
    spread_rows(my_c, q, g, o, q_rows, g_rows, q_cols, g_cols, deltas)

    low_group = order[2 * rank]
    high_group = order[2 * rank + 1]
    high_blocks = lax.div(high_group, BLOCK // GROUP) + 1

    def score_step(i, diagonal=False):
        is_low = (i >= high_blocks).astype(jnp.int32)
        block = i - is_low * high_blocks
        row0 = pl.multiple_of((1 - is_low) * rows, rows)
        key0 = pl.multiple_of(block * BLOCK, BLOCK)
        key_tile = keys[:, pl.ds(key0, BLOCK)]
        t = mm(q_rows[pl.ds(row0, rows), :], key_tile) * log2_scale
        dweights[i] = mm(g_rows[pl.ds(row0, rows), :], key_tile[:LATENT])
        if diagonal:
            group = jnp.where(is_low == 1, low_group, high_group)
            token = lax.broadcasted_iota(jnp.int32, (rows, BLOCK), 0) % GROUP
            lane = lax.broadcasted_iota(jnp.int32, (rows, BLOCK), 1)
            t = jnp.where(lane - token <= group * GROUP - block * BLOCK, t, neg_fill)
        scores[i] = t
        left, right = t[:, : BLOCK // 2], t[:, BLOCK // 2 :]
        old_top = top[pl.ds(row0, rows), :]
        new_top = jnp.maximum(old_top, jnp.maximum(left, right))
        added = jnp.exp2(left - new_top) + jnp.exp2(right - new_top)
        total[pl.ds(row0, rows), :] = total[pl.ds(row0, rows), :] * jnp.exp2(old_top - new_top) + added
        top[pl.ds(row0, rows), :] = new_top

    def whole(k):
        score_step(k + (k >= high_blocks - 1).astype(jnp.int32))

    def whole_pair(j, carry):
        whole(2 * j + 1)
        whole(2 * j + 2)
        return carry

    score_step(high_blocks - 1, diagonal=True)
    score_step(jnp.int32(items - 1), diagonal=True)
    whole(jnp.int32(0))
    lax.fori_loop(0, (items - 3) // 2, whole_pair, 0)

    lane_top = top[...]
    row_top = jnp.max(lane_top, axis=1, keepdims=True)
    row_sum = jnp.sum(total[...] * jnp.exp2(lane_top - row_top), axis=1, keepdims=True)
    top[...] = jnp.broadcast_to(row_top + jnp.log2(row_sum), top.shape)

    def weigh(i):
        row0 = pl.multiple_of((i < high_blocks).astype(jnp.int32) * rows, rows)
        w = jnp.exp2(scores[i] - twice(top[pl.ds(row0, rows), :]))
        ds = w * (dweights[i] - twice(deltas[pl.ds(row0, rows), :])) * score_scale
        ds = ds.astype(jnp.bfloat16)
        dscores[i] = ds
        return ds, w.astype(jnp.bfloat16)

    key_sums(
        order, q_cols, g_cols, slot_of, keep, send, weigh, sides=sides, rows=rows
    )


def query_kernel(order, dscores, keys, out, acc, *, sides, rows):
    items = dscores.shape[0]
    my_x, my_y, my_c = here()
    rank = (my_x * sides + my_y) * 2 + my_c
    high_blocks = lax.div(order[2 * rank + 1], BLOCK // GROUP) + 1
    low_blocks = items - high_blocks
    acc[...] = jnp.zeros(acc.shape, jnp.float32)

    def term(i, key0):
        key0 = pl.multiple_of(key0, BLOCK)
        return lax.dot_general(
            dscores[i], keys[:, pl.ds(key0, BLOCK)], NT, preferred_element_type=jnp.float32
        )

    def high(j, carry):
        acc[rows:, :] += term(2 * j, 2 * j * BLOCK) + term(2 * j + 1, (2 * j + 1) * BLOCK)
        return carry

    def low(j, carry):
        i = high_blocks + 2 * j
        acc[:rows, :] += term(i, 2 * j * BLOCK) + term(i + 1, (2 * j + 1) * BLOCK)
        return carry

    lax.fori_loop(0, lax.div(high_blocks, 2), high, 0)
    lax.fori_loop(0, lax.div(low_blocks, 2), low, 0)
    odd_high = lax.rem(high_blocks, 2)
    row0 = pl.multiple_of(odd_high * rows, rows)
    block = jnp.where(odd_high == 1, high_blocks, low_blocks) - 1
    last = block + (1 - odd_high) * high_blocks
    acc[pl.ds(row0, rows), :] += term(last, block * BLOCK)

    tokens = out.shape[0] // 2
    heads = rows // tokens
    for half in range(2):
        for head in range(heads):
            at = (half * heads + head) * tokens
            out[half * tokens : (half + 1) * tokens, head * WIDTH : (head + 1) * WIDTH] = acc[
                at : at + tokens, :
            ].astype(jnp.bfloat16)


def run_grads(order, q, g, o, pieces, sides):
    rows = q.shape[0] * q.shape[1] // WIDTH // 2
    pairs = 2 * sides * sides
    items = pairs * PAIR // BLOCK + 1
    vmem = pl.BlockSpec(memory_space=pltpu.VMEM)
    smem = pl.BlockSpec(memory_space=pltpu.SMEM)
    hbm = pl.BlockSpec(memory_space=pl.ANY)
    bf16, f32 = jnp.bfloat16, jnp.float32
    part = pltpu.VMEM((sides, sides, 2, HALF, PAIR), bf16)
    return pl.pallas_call(
        functools.partial(grads_kernel, sides=sides, rows=rows),
        out_shape=(
            pltpu.VMEM((WIDTH, pairs * PAIR), bf16),
            pltpu.VMEM((items, rows, BLOCK), bf16),
            part,
            part,
        ),
        in_specs=[smem] + [hbm] * 3 + [vmem] * len(pieces),
        out_specs=(vmem,) * 4,
        scratch_shapes=[
            pltpu.VMEM((items, rows, BLOCK), f32),
            pltpu.VMEM((items, rows, BLOCK), f32),
            pltpu.VMEM((2 * rows, 128), f32),
            pltpu.VMEM((2 * rows, 128), f32),
            pltpu.VMEM(q.shape, bf16),
            pltpu.VMEM(g.shape, bf16),
            pltpu.VMEM(o.shape, bf16),
            pltpu.VMEM((2 * rows, WIDTH), bf16),
            pltpu.VMEM((2 * rows, LATENT), bf16),
            pltpu.VMEM((WIDTH, 2 * rows), bf16),
            pltpu.VMEM((WIDTH, 2 * rows), bf16),
            pltpu.VMEM((2 * rows, 128), f32),
            pltpu.SMEM((2 * pairs,), jnp.int32),
            pltpu.SemaphoreType.DMA((3,)),
        ],
        compiler_params=pltpu.CompilerParams(vmem_limit_bytes=38 * 1024 * 1024),
        cost_estimate=pl.CostEstimate(
            flops=items * rows * BLOCK * 2 * 2176, bytes_accessed=24 << 20, transcendentals=0
        ),
        name="latent_grads",
    )(order, q, g, o, *[on_chip(a) for a in pieces])


def run_queries(order, dscores, keys, sides, out_shape):
    items, rows = dscores.shape[:2]
    vmem = pl.BlockSpec(memory_space=pltpu.VMEM)
    smem = pl.BlockSpec(memory_space=pltpu.SMEM)
    return pl.pallas_call(
        functools.partial(query_kernel, sides=sides, rows=rows),
        out_shape=jax.ShapeDtypeStruct(out_shape, jnp.bfloat16),
        in_specs=[smem, vmem, vmem],
        out_specs=vmem,
        scratch_shapes=[pltpu.VMEM((2 * rows, WIDTH), jnp.float32)],
        compiler_params=pltpu.CompilerParams(vmem_limit_bytes=24 * 1024 * 1024),
        cost_estimate=pl.CostEstimate(
            flops=items * rows * BLOCK * 2 * WIDTH, bytes_accessed=10 << 20, transcendentals=0
        ),
        name="latent_queries",
    )(order, on_chip(dscores), on_chip(keys))


def hop(a, sides, stage, step):
    moves = []
    for x in range(sides):
        for y in range(sides):
            for c in range(2):
                along_y = stage == c
                from_x = x if along_y else (x + step) % sides
                from_y = (y + step) % sides if along_y else y
                moves.append(((from_x * sides + from_y) * 2 + c, (x * sides + y) * 2 + c))
    return lax.ppermute(a, ("x", "y", "c"), moves)


def swap(a):
    return lax.ppermute(a, "c", [(0, 1), (1, 0)])


def shards(q_latent, kv_latent, out_grad, saved_out, group_order, *, sides, depth):
    mine, theirs = run_own(group_order, kv_latent.T, sides)
    both = jnp.stack([mine, swap(theirs)])
    line = jnp.stack([both] + [hop(both, sides, 0, d) for d in range(1, sides)])
    far = [hop(line, sides, 1, d) for d in range(1, sides)]
    pieces = [line] + far
    pieces = pieces + [swap(piece) for piece in pieces]

    keys, dscores, keep, send = run_grads(
        group_order, q_latent, out_grad, saved_out, pieces, sides
    )
    total = keep.astype(jnp.float32) + swap(send).astype(jnp.float32)
    low = [total[d].astype(jnp.bfloat16) for d in range(1, sides)]
    low, dscores = lax.optimization_barrier((low, dscores))
    q_grad = run_queries(group_order, dscores, keys, sides, q_latent.shape)
    total = total[0]
    for d in range(1, sides):
        total = total + hop(low[d - 1], sides, 1, -d).astype(jnp.float32)
    total, q_grad = lax.optimization_barrier((total, q_grad))
    low = [total[d].astype(jnp.bfloat16) for d in range(1, sides)]
    parts = [hop(low[d - 1], sides, 0, -d) for d in range(1, sides)]
    each = PAIR // depth
    by_owner = run_owner(group_order, total[0], parts, sides).reshape(2 * depth, each, HALF)
    parts = lax.all_to_all(by_owner, ("c", "z"), 0, 0, tiled=True)
    parts = jnp.sum(parts.astype(jnp.float32).reshape(2, depth, each, HALF), axis=1)
    return q_grad, jnp.concatenate([parts[0], parts[1]], axis=1)


def solution(mesh):
    ctx, depth = mesh.shape["ctx"], mesh.shape["head"]
    sides = math.isqrt(ctx // 2)
    finer = Mesh(mesh.devices.reshape(sides, sides, 2, depth), ("x", "y", "c", "z"))
    ctx_axes = ("x", "y", "c")
    placed = (P(ctx_axes, "z"), P(ctx_axes, None), P(ctx_axes, "z"), P(ctx_axes, "z"), P())
    return jax.shard_map(
        functools.partial(shards, sides=sides, depth=depth),
        mesh=finer,
        in_specs=placed,
        out_specs=(P(ctx_axes, "z"), P(("x", "y", "c", "z"), None)),
        check_vma=False,
    )
```

```python
import functools
import math

import jax
import jax.numpy as jnp
from jax import lax
from jax.experimental import pallas as pl
from jax.experimental.pallas import tpu as pltpu
from jax.sharding import Mesh, PartitionSpec as P

LATENT = 512
ROPE = 64
WIDTH = LATENT + ROPE
HALF = WIDTH // 2
GROUP = 64
BLOCK = 256
PAIR = 2 * GROUP

score_scale = 192.0 ** (-0.5)
log2_scale = score_scale * math.log2(math.e)
neg_fill = -1e30

NT = (((1,), (1,)), ((), ()))


def mm(a, b):
    return jnp.dot(a, b, preferred_element_type=jnp.float32)


def twice(a):
    return jnp.concatenate([a, a], axis=1)


def on_chip(a):
    return pltpu.with_memory_space_constraint(a, pltpu.VMEM)


def here():
    return lax.axis_index("x"), lax.axis_index("y"), lax.axis_index("c")


def own_kernel(order, keys, out, *, sides):
    my_x, my_y, my_c = here()
    odd = lax.rem(order[2 * ((my_x * sides + my_y) * 2 + my_c)], 2)
    tile = keys[...]
    turned = jnp.concatenate([tile[:, GROUP:], tile[:, :GROUP]], axis=1)
    out[...] = jnp.where(odd == 1, turned, tile)


def run_own(order, keys, sides):
    vmem = pl.BlockSpec(memory_space=pltpu.VMEM)
    return pl.pallas_call(
        functools.partial(own_kernel, sides=sides),
        out_shape=jax.ShapeDtypeStruct(keys.shape, keys.dtype),
        in_specs=[pl.BlockSpec(memory_space=pltpu.SMEM), vmem],
        out_specs=vmem,
        name="latent_own",
    )(order, keys)


def owner_kernel(order, first, *rest, sides):
    parts, out = rest[:-1], rest[-1]
    my_x, my_y, _ = here()
    for core in range(2):
        total = first[core]
        for part in parts:
            total = total + part[core].astype(jnp.float32)
        odd = lax.rem(order[2 * ((my_x * sides + my_y) * 2 + core)], 2)
        turned = jnp.concatenate([total[:, GROUP:], total[:, :GROUP]], axis=1)
        total = jnp.where(odd == 1, turned, total)
        out[core * PAIR : (core + 1) * PAIR, :] = total.astype(jnp.bfloat16).T


def run_owner(order, first, parts, sides):
    vmem = pl.BlockSpec(memory_space=pltpu.VMEM)
    return pl.pallas_call(
        functools.partial(owner_kernel, sides=sides),
        out_shape=jax.ShapeDtypeStruct((2 * PAIR, HALF), jnp.bfloat16),
        in_specs=[pl.BlockSpec(memory_space=pltpu.SMEM)] + [vmem] * (1 + len(parts)),
        out_specs=vmem,
        name="latent_owner",
    )(order, *[on_chip(a) for a in (first, *parts)])


def key_sums(order, q_cols, g_cols, slot_of, keep, send, weigh, *, sides, rows):
    groups = 4 * sides * sides
    per_block = BLOCK // GROUP
    blocks = groups // per_block
    my_x, my_y, my_c = here()
    rank = (my_x * sides + my_y) * 2 + my_c
    high_blocks = lax.div(order[2 * rank + 1], per_block) + 1
    low_blocks = blocks + 1 - high_blocks

    def term(i, half):
        dscores, weights = weigh(i)
        at = half * rows
        return mm(q_cols[:, at : at + rows], dscores) + mm(g_cols[:, at : at + rows], weights)

    def put(b, tile):
        tile = tile.astype(jnp.bfloat16)
        for j in range(per_block):
            p = slot_of[b * per_block + j]
            step_x = lax.rem(lax.div(p, 2 * sides) - my_x + sides, sides)
            step_y = lax.rem(lax.rem(lax.div(p, 2), sides) - my_y + sides, sides)
            step1 = jnp.where(my_c == 0, step_x, step_y)
            step2 = jnp.where(my_c == 0, step_y, step_x)
            core = lax.rem(p, 2)
            lanes = pl.ds(j % 2 * GROUP, GROUP)
            keep[step1, step2, core, :, lanes] = tile[:HALF, j * GROUP : (j + 1) * GROUP]
            send[step2, step1, core, :, lanes] = tile[HALF:, j * GROUP : (j + 1) * GROUP]

    def both(b, carry):
        high = term(b, 1)
        put(b, high + term(high_blocks + b, 0))
        return carry

    def two(j, carry):
        b = low_blocks + 1 + 2 * j
        first = term(b, 1)
        second = term(b + 1, 1)
        put(b, first)
        put(b + 1, second)
        return carry

    def clear(b, carry):
        put(b, jnp.zeros((WIDTH, BLOCK), jnp.float32))
        return carry

    lax.fori_loop(0, low_blocks, both, 0)
    put(low_blocks, term(low_blocks, 1))
    lax.fori_loop(0, lax.div(high_blocks - low_blocks - 1, 2), two, 0)
    lax.fori_loop(high_blocks, blocks, clear, 0)


def spread_rows(core, q, g, o, q_rows, g_rows, q_cols, g_cols, deltas):
    tokens = q.shape[0] // 2
    heads = q.shape[1] // WIDTH
    for half in range(2):
        for head in range(heads):
            at = (half * heads + head) * tokens
            own = slice(half * tokens, half * tokens + tokens)
            grads = g[own, head * LATENT : (head + 1) * LATENT]
            saved = o[own, head * LATENT : (head + 1) * LATENT]
            q_rows[at : at + tokens, :] = q[own, head * WIDTH : (head + 1) * WIDTH]
            g_rows[at : at + tokens, :] = grads
            delta = jnp.sum(grads.astype(jnp.float32) * saved.astype(jnp.float32), axis=1, keepdims=True)
            deltas[at : at + tokens, :] = jnp.broadcast_to(delta, (tokens, 128))
    first = pl.multiple_of(core * HALF, HALF)
    second = pl.multiple_of((1 - core) * HALF, HALF)
    g_cols[pl.ds(second, HALF), :] = jnp.zeros((HALF, g_cols.shape[1]), jnp.bfloat16)
    for at in range(0, 2 * heads * tokens, 128):
        q_turned = q_rows[at : at + 128, :].T
        g_turned = g_rows[at : at + 128, :].T
        q_cols[pl.ds(first, HALF), at : at + 128] = q_turned[:HALF]
        q_cols[pl.ds(second, HALF), at : at + 128] = q_turned[HALF:]
        g_cols[pl.ds(first, HALF), at : at + 128] = g_turned[:HALF]
        g_cols[pl.ds(second, LATENT - HALF), at : at + 128] = g_turned[HALF:]


def grads_kernel(order, q_in, g_in, o_in, *rest, sides, rows):
    pieces = 2 * sides
    piece_refs = rest[:pieces]
    keys, dscores, keep, send = rest[pieces : pieces + 4]
    (
        scores, dweights, top, total, q, g, o, q_rows, g_rows, q_cols, g_cols, deltas, slot_of,
        own_sem,
    ) = rest[pieces + 4 :]
    pairs = keys.shape[1] // PAIR
    groups = 2 * pairs
    blocks = groups * GROUP // BLOCK
    items = blocks + 1
    my_x, my_y, my_c = here()
    rank = (my_x * sides + my_y) * 2 + my_c

    own = [
        pltpu.make_async_copy(src, dst, own_sem.at[at])
        for at, (src, dst) in enumerate([(q_in, q), (g_in, g), (o_in, o)])
    ]
    for copy in own:
        copy.start()
    def note(p, carry):
        slot_of[order[2 * p]] = p
        slot_of[order[2 * p + 1]] = p
        return carry

    lax.fori_loop(0, pairs, note, 0)
    top[...] = jnp.full(top.shape, neg_fill, jnp.float32)
    total[...] = jnp.zeros(total.shape, jnp.float32)

    for at, ref in enumerate(piece_refs):
        step2 = at % sides
        holder = my_c if at < sides else 1 - my_c
        for step1 in range(sides):
            at_x = lax.rem(my_x + jnp.where(holder == 0, step2, step1), sides)
            at_y = lax.rem(my_y + jnp.where(holder == 0, step1, step2), sides)
            pair = (at_x * sides + at_y) * 2 + holder
            tile = ref[step1]
            turn = lax.rem(order[2 * pair], 2)
            even = lax.div(order[2 * pair + turn], 2) * PAIR
            odd = lax.div(order[2 * pair + 1 - turn], 2) * PAIR
            evens = keys.at[:, pl.ds(pl.multiple_of(even, PAIR), PAIR)]
            odds = keys.at[:, pl.ds(pl.multiple_of(odd, PAIR), PAIR)]
            evens[:, :GROUP] = tile[:, :GROUP]
            odds[:, GROUP:] = tile[:, GROUP:]
    for copy in own:
        copy.wait()
    spread_rows(my_c, q, g, o, q_rows, g_rows, q_cols, g_cols, deltas)

    low_group = order[2 * rank]
    high_group = order[2 * rank + 1]
    high_blocks = lax.div(high_group, BLOCK // GROUP) + 1

    def score_step(i, diagonal=False):
        is_low = (i >= high_blocks).astype(jnp.int32)
        block = i - is_low * high_blocks
        row0 = pl.multiple_of((1 - is_low) * rows, rows)
        key0 = pl.multiple_of(block * BLOCK, BLOCK)
        key_tile = keys[:, pl.ds(key0, BLOCK)]
        t = mm(q_rows[pl.ds(row0, rows), :], key_tile) * log2_scale
        dweights[i] = mm(g_rows[pl.ds(row0, rows), :], key_tile[:LATENT])
        if diagonal:
            group = jnp.where(is_low == 1, low_group, high_group)
            token = lax.broadcasted_iota(jnp.int32, (rows, BLOCK), 0) % GROUP
            lane = lax.broadcasted_iota(jnp.int32, (rows, BLOCK), 1)
            t = jnp.where(lane - token <= group * GROUP - block * BLOCK, t, neg_fill)
        scores[i] = t
        left, right = t[:, : BLOCK // 2], t[:, BLOCK // 2 :]
        old_top = top[pl.ds(row0, rows), :]
        new_top = jnp.maximum(old_top, jnp.maximum(left, right))
        added = jnp.exp2(left - new_top) + jnp.exp2(right - new_top)
        total[pl.ds(row0, rows), :] = total[pl.ds(row0, rows), :] * jnp.exp2(old_top - new_top) + added
        top[pl.ds(row0, rows), :] = new_top

    def whole(k):
        score_step(k + (k >= high_blocks - 1).astype(jnp.int32))

    def whole_pair(j, carry):
        whole(2 * j + 1)
        whole(2 * j + 2)
        return carry

    score_step(high_blocks - 1, diagonal=True)
    score_step(jnp.int32(items - 1), diagonal=True)
    whole(jnp.int32(0))
    lax.fori_loop(0, (items - 3) // 2, whole_pair, 0)

    lane_top = top[...]
    row_top = jnp.max(lane_top, axis=1, keepdims=True)
    row_sum = jnp.sum(total[...] * jnp.exp2(lane_top - row_top), axis=1, keepdims=True)
    top[...] = jnp.broadcast_to(row_top + jnp.log2(row_sum), top.shape)

    def weigh(i):
        row0 = pl.multiple_of((i < high_blocks).astype(jnp.int32) * rows, rows)
        w = jnp.exp2(scores[i] - twice(top[pl.ds(row0, rows), :]))
        ds = w * (dweights[i] - twice(deltas[pl.ds(row0, rows), :])) * score_scale
        ds = ds.astype(jnp.bfloat16)
        dscores[i] = ds
        return ds, w.astype(jnp.bfloat16)

    key_sums(
        order, q_cols, g_cols, slot_of, keep, send, weigh, sides=sides, rows=rows
    )


def query_kernel(order, dscores, keys, out, acc, *, sides, rows):
    items = dscores.shape[0]
    my_x, my_y, my_c = here()
    rank = (my_x * sides + my_y) * 2 + my_c
    high_blocks = lax.div(order[2 * rank + 1], BLOCK // GROUP) + 1
    low_blocks = items - high_blocks
    acc[...] = jnp.zeros(acc.shape, jnp.float32)

    def term(i, key0):
        key0 = pl.multiple_of(key0, BLOCK)
        return lax.dot_general(
            dscores[i], keys[:, pl.ds(key0, BLOCK)], NT, preferred_element_type=jnp.float32
        )

    def high(j, carry):
        acc[rows:, :] += term(2 * j, 2 * j * BLOCK) + term(2 * j + 1, (2 * j + 1) * BLOCK)
        return carry

    def low(j, carry):
        i = high_blocks + 2 * j
        acc[:rows, :] += term(i, 2 * j * BLOCK) + term(i + 1, (2 * j + 1) * BLOCK)
        return carry

    lax.fori_loop(0, lax.div(high_blocks, 2), high, 0)
    lax.fori_loop(0, lax.div(low_blocks, 2), low, 0)
    odd_high = lax.rem(high_blocks, 2)
    row0 = pl.multiple_of(odd_high * rows, rows)
    block = jnp.where(odd_high == 1, high_blocks, low_blocks) - 1
    last = block + (1 - odd_high) * high_blocks
    acc[pl.ds(row0, rows), :] += term(last, block * BLOCK)

    tokens = out.shape[0] // 2
    heads = rows // tokens
    for half in range(2):
        for head in range(heads):
            at = (half * heads + head) * tokens
            out[half * tokens : (half + 1) * tokens, head * WIDTH : (head + 1) * WIDTH] = acc[
                at : at + tokens, :
            ].astype(jnp.bfloat16)


def run_grads(order, q, g, o, pieces, sides):
    rows = q.shape[0] * q.shape[1] // WIDTH // 2
    pairs = 2 * sides * sides
    items = pairs * PAIR // BLOCK + 1
    vmem = pl.BlockSpec(memory_space=pltpu.VMEM)
    smem = pl.BlockSpec(memory_space=pltpu.SMEM)
    hbm = pl.BlockSpec(memory_space=pl.ANY)
    bf16, f32 = jnp.bfloat16, jnp.float32
    part = pltpu.VMEM((sides, sides, 2, HALF, PAIR), bf16)
    return pl.pallas_call(
        functools.partial(grads_kernel, sides=sides, rows=rows),
        out_shape=(
            pltpu.VMEM((WIDTH, pairs * PAIR), bf16),
            pltpu.VMEM((items, rows, BLOCK), bf16),
            part,
            part,
        ),
        in_specs=[smem] + [hbm] * 3 + [vmem] * len(pieces),
        out_specs=(vmem,) * 4,
        scratch_shapes=[
            pltpu.VMEM((items, rows, BLOCK), f32),
            pltpu.VMEM((items, rows, BLOCK), f32),
            pltpu.VMEM((2 * rows, 128), f32),
            pltpu.VMEM((2 * rows, 128), f32),
            pltpu.VMEM(q.shape, bf16),
            pltpu.VMEM(g.shape, bf16),
            pltpu.VMEM(o.shape, bf16),
            pltpu.VMEM((2 * rows, WIDTH), bf16),
            pltpu.VMEM((2 * rows, LATENT), bf16),
            pltpu.VMEM((WIDTH, 2 * rows), bf16),
            pltpu.VMEM((WIDTH, 2 * rows), bf16),
            pltpu.VMEM((2 * rows, 128), f32),
            pltpu.SMEM((2 * pairs,), jnp.int32),
            pltpu.SemaphoreType.DMA((3,)),
        ],
        compiler_params=pltpu.CompilerParams(vmem_limit_bytes=38 * 1024 * 1024),
        cost_estimate=pl.CostEstimate(
            flops=items * rows * BLOCK * 2 * 2176, bytes_accessed=24 << 20, transcendentals=0
        ),
        name="latent_grads",
    )(order, q, g, o, *[on_chip(a) for a in pieces])


def run_queries(order, dscores, keys, sides, out_shape):
    items, rows = dscores.shape[:2]
    vmem = pl.BlockSpec(memory_space=pltpu.VMEM)
    smem = pl.BlockSpec(memory_space=pltpu.SMEM)
    return pl.pallas_call(
        functools.partial(query_kernel, sides=sides, rows=rows),
        out_shape=jax.ShapeDtypeStruct(out_shape, jnp.bfloat16),
        in_specs=[smem, vmem, vmem],
        out_specs=vmem,
        scratch_shapes=[pltpu.VMEM((2 * rows, WIDTH), jnp.float32)],
        compiler_params=pltpu.CompilerParams(vmem_limit_bytes=24 * 1024 * 1024),
        cost_estimate=pl.CostEstimate(
            flops=items * rows * BLOCK * 2 * WIDTH, bytes_accessed=10 << 20, transcendentals=0
        ),
        name="latent_queries",
    )(order, on_chip(dscores), on_chip(keys))


def hop(a, sides, stage, step):
    moves = []
    for x in range(sides):
        for y in range(sides):
            for c in range(2):
                along_y = stage == c
                from_x = x if along_y else (x + step) % sides
                from_y = (y + step) % sides if along_y else y
                moves.append(((from_x * sides + from_y) * 2 + c, (x * sides + y) * 2 + c))
    return lax.ppermute(a, ("x", "y", "c"), moves)


def swap(a):
    return lax.ppermute(a, "c", [(0, 1), (1, 0)])


def shards(q_latent, kv_latent, out_grad, saved_out, group_order, *, sides, depth):
    own = run_own(group_order, kv_latent.T, sides)
    line = jnp.stack([own] + [hop(own, sides, 0, d) for d in range(1, sides)])
    far = [hop(line, sides, 1, d) for d in range(1, sides)]
    pieces = [line] + far
    pieces = pieces + [swap(piece) for piece in pieces]

    keys, dscores, keep, send = run_grads(
        group_order, q_latent, out_grad, saved_out, pieces, sides
    )
    both = {}
    for d in sorted(range(sides), key=lambda d: -min(d, sides - d)):
        both[d] = keep[d].astype(jnp.float32) + swap(send[d]).astype(jnp.float32)
    low = [both[d].astype(jnp.bfloat16) for d in range(1, sides)]
    low, dscores = lax.optimization_barrier((low, dscores))
    q_grad = run_queries(group_order, dscores, keys, sides, q_latent.shape)
    total = both[0]
    for d in range(1, sides):
        total = total + hop(low[d - 1], sides, 1, -d).astype(jnp.float32)
    total, q_grad = lax.optimization_barrier((total, q_grad))
    low = [total[d].astype(jnp.bfloat16) for d in range(1, sides)]
    parts = [hop(low[d - 1], sides, 0, -d) for d in range(1, sides)]
    each = PAIR // depth
    by_owner = run_owner(group_order, total[0], parts, sides).reshape(2 * depth, each, HALF)
    parts = lax.all_to_all(by_owner, ("c", "z"), 0, 0, tiled=True)
    parts = jnp.sum(parts.astype(jnp.float32).reshape(2, depth, each, HALF), axis=1)
    return q_grad, jnp.concatenate([parts[0], parts[1]], axis=1)


def solution(mesh):
    ctx, depth = mesh.shape["ctx"], mesh.shape["head"]
    sides = math.isqrt(ctx // 2)
    finer = Mesh(mesh.devices.reshape(sides, sides, 2, depth), ("x", "y", "c", "z"))
    ctx_axes = ("x", "y", "c")
    placed = (P(ctx_axes, "z"), P(ctx_axes, None), P(ctx_axes, "z"), P(ctx_axes, "z"), P())
    return jax.shard_map(
        functools.partial(shards, sides=sides, depth=depth),
        mesh=finer,
        in_specs=placed,
        out_specs=(P(ctx_axes, "z"), P(("x", "y", "c", "z"), None)),
        check_vma=False,
    )
```

```python
import functools
import math

import jax
import jax.numpy as jnp
from jax import lax
from jax.experimental import pallas as pl
from jax.experimental.pallas import tpu as pltpu
from jax.sharding import Mesh, PartitionSpec as P

LATENT = 512
ROPE = 64
WIDTH = LATENT + ROPE
HALF = WIDTH // 2
GROUP = 64
BLOCK = 256
PAIR = 2 * GROUP

score_scale = 192.0 ** (-0.5)
log2_scale = score_scale * math.log2(math.e)
neg_fill = -1e30

NT = (((1,), (1,)), ((), ()))


def mm(a, b):
    return jnp.dot(a, b, preferred_element_type=jnp.float32)


def twice(a):
    return jnp.concatenate([a, a], axis=1)


def on_chip(a):
    return pltpu.with_memory_space_constraint(a, pltpu.VMEM)


def here():
    return lax.axis_index("x"), lax.axis_index("y"), lax.axis_index("c")


def own_kernel(order, keys, out, *, sides):
    my_x, my_y, my_c = here()
    odd = lax.rem(order[2 * ((my_x * sides + my_y) * 2 + my_c)], 2)
    tile = keys[...]
    turned = jnp.concatenate([tile[:, GROUP:], tile[:, :GROUP]], axis=1)
    out[...] = jnp.where(odd == 1, turned, tile)


def run_own(order, keys, sides):
    vmem = pl.BlockSpec(memory_space=pltpu.VMEM)
    return pl.pallas_call(
        functools.partial(own_kernel, sides=sides),
        out_shape=jax.ShapeDtypeStruct(keys.shape, keys.dtype),
        in_specs=[pl.BlockSpec(memory_space=pltpu.SMEM), vmem],
        out_specs=vmem,
        name="latent_own",
    )(order, keys)


def owner_kernel(order, first, *rest, sides):
    parts, out = rest[:-1], rest[-1]
    my_x, my_y, _ = here()
    for core in range(2):
        total = first[core]
        for part in parts:
            total = total + part[core].astype(jnp.float32)
        odd = lax.rem(order[2 * ((my_x * sides + my_y) * 2 + core)], 2)
        turned = jnp.concatenate([total[:, GROUP:], total[:, :GROUP]], axis=1)
        total = jnp.where(odd == 1, turned, total)
        out[core * PAIR : (core + 1) * PAIR, :] = total.astype(jnp.bfloat16).T


def run_owner(order, first, parts, sides):
    vmem = pl.BlockSpec(memory_space=pltpu.VMEM)
    return pl.pallas_call(
        functools.partial(owner_kernel, sides=sides),
        out_shape=jax.ShapeDtypeStruct((2 * PAIR, HALF), jnp.bfloat16),
        in_specs=[pl.BlockSpec(memory_space=pltpu.SMEM)] + [vmem] * (1 + len(parts)),
        out_specs=vmem,
        name="latent_owner",
    )(order, *[on_chip(a) for a in (first, *parts)])


def key_sums(order, q_cols, g_cols, slot_of, keep, send, weigh, *, sides, rows):
    groups = 4 * sides * sides
    per_block = BLOCK // GROUP
    blocks = groups // per_block
    my_x, my_y, my_c = here()
    rank = (my_x * sides + my_y) * 2 + my_c
    high_blocks = lax.div(order[2 * rank + 1], per_block) + 1
    low_blocks = blocks + 1 - high_blocks

    def term(i, half):
        dscores, weights = weigh(i)
        at = half * rows
        return mm(q_cols[:, at : at + rows], dscores) + mm(g_cols[:, at : at + rows], weights)

    def put(b, tile):
        tile = tile.astype(jnp.bfloat16)
        for j in range(per_block):
            p = slot_of[b * per_block + j]
            step_x = lax.rem(lax.div(p, 2 * sides) - my_x + sides, sides)
            step_y = lax.rem(lax.rem(lax.div(p, 2), sides) - my_y + sides, sides)
            step1 = jnp.where(my_c == 0, step_x, step_y)
            step2 = jnp.where(my_c == 0, step_y, step_x)
            core = lax.rem(p, 2)
            lanes = pl.ds(j % 2 * GROUP, GROUP)
            keep[step1, step2, core, :, lanes] = tile[:HALF, j * GROUP : (j + 1) * GROUP]
            send[step2, step1, core, :, lanes] = tile[HALF:, j * GROUP : (j + 1) * GROUP]

    def both(b, carry):
        high = term(b, 1)
        put(b, high + term(high_blocks + b, 0))
        return carry

    def two(j, carry):
        b = low_blocks + 1 + 2 * j
        first = term(b, 1)
        second = term(b + 1, 1)
        put(b, first)
        put(b + 1, second)
        return carry

    def clear(b, carry):
        put(b, jnp.zeros((WIDTH, BLOCK), jnp.float32))
        return carry

    lax.fori_loop(0, low_blocks, both, 0)
    put(low_blocks, term(low_blocks, 1))
    lax.fori_loop(0, lax.div(high_blocks - low_blocks - 1, 2), two, 0)
    lax.fori_loop(high_blocks, blocks, clear, 0)


def spread_rows(core, q, g, o, q_rows, g_rows, q_cols, g_cols, deltas):
    tokens = q.shape[0] // 2
    heads = q.shape[1] // WIDTH
    for half in range(2):
        for head in range(heads):
            at = (half * heads + head) * tokens
            own = slice(half * tokens, half * tokens + tokens)
            grads = g[own, head * LATENT : (head + 1) * LATENT]
            saved = o[own, head * LATENT : (head + 1) * LATENT]
            q_rows[at : at + tokens, :] = q[own, head * WIDTH : (head + 1) * WIDTH]
            g_rows[at : at + tokens, :] = grads
            delta = jnp.sum(grads.astype(jnp.float32) * saved.astype(jnp.float32), axis=1, keepdims=True)
            deltas[at : at + tokens, :] = jnp.broadcast_to(delta, (tokens, 128))
    first = pl.multiple_of(core * HALF, HALF)
    second = pl.multiple_of((1 - core) * HALF, HALF)
    g_cols[pl.ds(second, HALF), :] = jnp.zeros((HALF, g_cols.shape[1]), jnp.bfloat16)
    for at in range(0, 2 * heads * tokens, 128):
        q_turned = q_rows[at : at + 128, :].T
        g_turned = g_rows[at : at + 128, :].T
        q_cols[pl.ds(first, HALF), at : at + 128] = q_turned[:HALF]
        q_cols[pl.ds(second, HALF), at : at + 128] = q_turned[HALF:]
        g_cols[pl.ds(first, HALF), at : at + 128] = g_turned[:HALF]
        g_cols[pl.ds(second, LATENT - HALF), at : at + 128] = g_turned[HALF:]


def grads_kernel(order, q_in, g_in, o_in, *rest, sides, rows):
    pieces = 2 * sides
    piece_refs = rest[:pieces]
    keys, dscores, keep, send = rest[pieces : pieces + 4]
    (
        scores, dweights, top, total, q, g, o, q_rows, g_rows, q_cols, g_cols, deltas, slot_of,
        own_sem,
    ) = rest[pieces + 4 :]
    pairs = keys.shape[1] // PAIR
    groups = 2 * pairs
    blocks = groups * GROUP // BLOCK
    items = blocks + 1
    my_x, my_y, my_c = here()
    rank = (my_x * sides + my_y) * 2 + my_c

    own = [
        pltpu.make_async_copy(src, dst, own_sem.at[at])
        for at, (src, dst) in enumerate([(q_in, q), (g_in, g), (o_in, o)])
    ]
    for copy in own:
        copy.start()
    def note(p, carry):
        slot_of[order[2 * p]] = p
        slot_of[order[2 * p + 1]] = p
        return carry

    lax.fori_loop(0, pairs, note, 0)
    top[...] = jnp.full(top.shape, neg_fill, jnp.float32)
    total[...] = jnp.zeros(total.shape, jnp.float32)

    for at, ref in enumerate(piece_refs):
        step2 = at % sides
        holder = my_c if at < sides else 1 - my_c
        for step1 in range(sides):
            at_x = lax.rem(my_x + jnp.where(holder == 0, step2, step1), sides)
            at_y = lax.rem(my_y + jnp.where(holder == 0, step1, step2), sides)
            pair = (at_x * sides + at_y) * 2 + holder
            tile = ref[step1]
            turn = lax.rem(order[2 * pair], 2)
            even = lax.div(order[2 * pair + turn], 2) * PAIR
            odd = lax.div(order[2 * pair + 1 - turn], 2) * PAIR
            evens = keys.at[:, pl.ds(pl.multiple_of(even, PAIR), PAIR)]
            odds = keys.at[:, pl.ds(pl.multiple_of(odd, PAIR), PAIR)]
            evens[:, :GROUP] = tile[:, :GROUP]
            odds[:, GROUP:] = tile[:, GROUP:]
    for copy in own:
        copy.wait()
    spread_rows(my_c, q, g, o, q_rows, g_rows, q_cols, g_cols, deltas)

    low_group = order[2 * rank]
    high_group = order[2 * rank + 1]
    high_blocks = lax.div(high_group, BLOCK // GROUP) + 1

    def score_step(i, diagonal=False):
        is_low = (i >= high_blocks).astype(jnp.int32)
        block = i - is_low * high_blocks
        row0 = pl.multiple_of((1 - is_low) * rows, rows)
        key0 = pl.multiple_of(block * BLOCK, BLOCK)
        key_tile = keys[:, pl.ds(key0, BLOCK)]
        t = mm(q_rows[pl.ds(row0, rows), :], key_tile) * log2_scale
        dweights[i] = mm(g_rows[pl.ds(row0, rows), :], key_tile[:LATENT])
        if diagonal:
            group = jnp.where(is_low == 1, low_group, high_group)
            token = lax.broadcasted_iota(jnp.int32, (rows, BLOCK), 0) % GROUP
            lane = lax.broadcasted_iota(jnp.int32, (rows, BLOCK), 1)
            t = jnp.where(lane - token <= group * GROUP - block * BLOCK, t, neg_fill)
        scores[i] = t
        left, right = t[:, : BLOCK // 2], t[:, BLOCK // 2 :]
        old_top = top[pl.ds(row0, rows), :]
        new_top = jnp.maximum(old_top, jnp.maximum(left, right))
        added = jnp.exp2(left - new_top) + jnp.exp2(right - new_top)
        total[pl.ds(row0, rows), :] = total[pl.ds(row0, rows), :] * jnp.exp2(old_top - new_top) + added
        top[pl.ds(row0, rows), :] = new_top

    def whole(k):
        score_step(k + (k >= high_blocks - 1).astype(jnp.int32))

    def whole_pair(j, carry):
        whole(2 * j + 1)
        whole(2 * j + 2)
        return carry

    score_step(high_blocks - 1, diagonal=True)
    score_step(jnp.int32(items - 1), diagonal=True)
    whole(jnp.int32(0))
    lax.fori_loop(0, (items - 3) // 2, whole_pair, 0)

    lane_top = top[...]
    row_top = jnp.max(lane_top, axis=1, keepdims=True)
    row_sum = jnp.sum(total[...] * jnp.exp2(lane_top - row_top), axis=1, keepdims=True)
    top[...] = jnp.broadcast_to(row_top + jnp.log2(row_sum), top.shape)

    def weigh(i):
        row0 = pl.multiple_of((i < high_blocks).astype(jnp.int32) * rows, rows)
        w = jnp.exp2(scores[i] - twice(top[pl.ds(row0, rows), :]))
        ds = w * (dweights[i] - twice(deltas[pl.ds(row0, rows), :])) * score_scale
        ds = ds.astype(jnp.bfloat16)
        dscores[i] = ds
        return ds, w.astype(jnp.bfloat16)

    key_sums(
        order, q_cols, g_cols, slot_of, keep, send, weigh, sides=sides, rows=rows
    )


def query_kernel(order, dscores, keys, out, acc, *, sides, rows):
    items = dscores.shape[0]
    my_x, my_y, my_c = here()
    rank = (my_x * sides + my_y) * 2 + my_c
    high_blocks = lax.div(order[2 * rank + 1], BLOCK // GROUP) + 1
    low_blocks = items - high_blocks
    acc[...] = jnp.zeros(acc.shape, jnp.float32)

    def term(i, key0):
        key0 = pl.multiple_of(key0, BLOCK)
        return lax.dot_general(
            dscores[i], keys[:, pl.ds(key0, BLOCK)], NT, preferred_element_type=jnp.float32
        )

    def high(j, carry):
        acc[rows:, :] += term(2 * j, 2 * j * BLOCK) + term(2 * j + 1, (2 * j + 1) * BLOCK)
        return carry

    def low(j, carry):
        i = high_blocks + 2 * j
        acc[:rows, :] += term(i, 2 * j * BLOCK) + term(i + 1, (2 * j + 1) * BLOCK)
        return carry

    lax.fori_loop(0, lax.div(high_blocks, 2), high, 0)
    lax.fori_loop(0, lax.div(low_blocks, 2), low, 0)
    odd_high = lax.rem(high_blocks, 2)
    row0 = pl.multiple_of(odd_high * rows, rows)
    block = jnp.where(odd_high == 1, high_blocks, low_blocks) - 1
    last = block + (1 - odd_high) * high_blocks
    acc[pl.ds(row0, rows), :] += term(last, block * BLOCK)

    tokens = out.shape[0] // 2
    heads = rows // tokens
    for half in range(2):
        for head in range(heads):
            at = (half * heads + head) * tokens
            out[half * tokens : (half + 1) * tokens, head * WIDTH : (head + 1) * WIDTH] = acc[
                at : at + tokens, :
            ].astype(jnp.bfloat16)


def run_grads(order, q, g, o, pieces, sides):
    rows = q.shape[0] * q.shape[1] // WIDTH // 2
    pairs = 2 * sides * sides
    items = pairs * PAIR // BLOCK + 1
    vmem = pl.BlockSpec(memory_space=pltpu.VMEM)
    smem = pl.BlockSpec(memory_space=pltpu.SMEM)
    hbm = pl.BlockSpec(memory_space=pl.ANY)
    bf16, f32 = jnp.bfloat16, jnp.float32
    part = pltpu.VMEM((sides, sides, 2, HALF, PAIR), bf16)
    return pl.pallas_call(
        functools.partial(grads_kernel, sides=sides, rows=rows),
        out_shape=(
            pltpu.VMEM((WIDTH, pairs * PAIR), bf16),
            pltpu.VMEM((items, rows, BLOCK), bf16),
            part,
            part,
        ),
        in_specs=[smem] + [hbm] * 3 + [vmem] * len(pieces),
        out_specs=(vmem,) * 4,
        scratch_shapes=[
            pltpu.VMEM((items, rows, BLOCK), f32),
            pltpu.VMEM((items, rows, BLOCK), f32),
            pltpu.VMEM((2 * rows, 128), f32),
            pltpu.VMEM((2 * rows, 128), f32),
            pltpu.VMEM(q.shape, bf16),
            pltpu.VMEM(g.shape, bf16),
            pltpu.VMEM(o.shape, bf16),
            pltpu.VMEM((2 * rows, WIDTH), bf16),
            pltpu.VMEM((2 * rows, LATENT), bf16),
            pltpu.VMEM((WIDTH, 2 * rows), bf16),
            pltpu.VMEM((WIDTH, 2 * rows), bf16),
            pltpu.VMEM((2 * rows, 128), f32),
            pltpu.SMEM((2 * pairs,), jnp.int32),
            pltpu.SemaphoreType.DMA((3,)),
        ],
        compiler_params=pltpu.CompilerParams(vmem_limit_bytes=38 * 1024 * 1024),
        cost_estimate=pl.CostEstimate(
            flops=items * rows * BLOCK * 2 * 2176, bytes_accessed=24 << 20, transcendentals=0
        ),
        name="latent_grads",
    )(order, q, g, o, *[on_chip(a) for a in pieces])


def run_queries(order, dscores, keys, sides, out_shape):
    items, rows = dscores.shape[:2]
    vmem = pl.BlockSpec(memory_space=pltpu.VMEM)
    smem = pl.BlockSpec(memory_space=pltpu.SMEM)
    return pl.pallas_call(
        functools.partial(query_kernel, sides=sides, rows=rows),
        out_shape=jax.ShapeDtypeStruct(out_shape, jnp.bfloat16),
        in_specs=[smem, vmem, vmem],
        out_specs=vmem,
        scratch_shapes=[pltpu.VMEM((2 * rows, WIDTH), jnp.float32)],
        compiler_params=pltpu.CompilerParams(vmem_limit_bytes=24 * 1024 * 1024),
        cost_estimate=pl.CostEstimate(
            flops=items * rows * BLOCK * 2 * WIDTH, bytes_accessed=10 << 20, transcendentals=0
        ),
        name="latent_queries",
    )(order, on_chip(dscores), on_chip(keys))


def hop(a, sides, stage, step):
    moves = []
    for x in range(sides):
        for y in range(sides):
            for c in range(2):
                along_y = stage == c
                from_x = x if along_y else (x + step) % sides
                from_y = (y + step) % sides if along_y else y
                moves.append(((from_x * sides + from_y) * 2 + c, (x * sides + y) * 2 + c))
    return lax.ppermute(a, ("x", "y", "c"), moves)


def swap(a):
    return lax.ppermute(a, "c", [(0, 1), (1, 0)])


def shards(q_latent, kv_latent, out_grad, saved_out, group_order, *, sides, depth):
    own = run_own(group_order, kv_latent.T, sides)
    line = jnp.stack([own] + [hop(own, sides, 0, d) for d in range(1, sides)])
    far = [hop(line, sides, 1, d) for d in range(1, sides)]
    pieces = [line] + far
    pieces = pieces + [swap(piece) for piece in pieces]

    keys, dscores, keep, send = run_grads(
        group_order, q_latent, out_grad, saved_out, pieces, sides
    )
    far_step = sides // 2
    others = [d for d in range(sides) if d != far_step]

    def add(d, sent):
        return keep[d].astype(jnp.float32) + swap(sent).astype(jnp.float32)

    both = {far_step: add(far_step, send[far_step])}
    low_far, sent = lax.optimization_barrier(
        (both[far_step].astype(jnp.bfloat16), [send[d] for d in others])
    )
    for d, part in zip(others, sent):
        both[d] = add(d, part)
    low = [low_far if d == far_step else both[d].astype(jnp.bfloat16) for d in range(1, sides)]
    low, dscores = lax.optimization_barrier((low, dscores))
    q_grad = run_queries(group_order, dscores, keys, sides, q_latent.shape)
    total = both[0]
    for d in range(1, sides):
        total = total + hop(low[d - 1], sides, 1, -d).astype(jnp.float32)
    total, q_grad = lax.optimization_barrier((total, q_grad))
    low = [total[d].astype(jnp.bfloat16) for d in range(1, sides)]
    parts = [hop(low[d - 1], sides, 0, -d) for d in range(1, sides)]
    each = PAIR // depth
    by_owner = run_owner(group_order, total[0], parts, sides).reshape(2 * depth, each, HALF)
    parts = lax.all_to_all(by_owner, ("c", "z"), 0, 0, tiled=True)
    parts = jnp.sum(parts.astype(jnp.float32).reshape(2, depth, each, HALF), axis=1)
    return q_grad, jnp.concatenate([parts[0], parts[1]], axis=1)


def solution(mesh):
    ctx, depth = mesh.shape["ctx"], mesh.shape["head"]
    sides = math.isqrt(ctx // 2)
    finer = Mesh(mesh.devices.reshape(sides, sides, 2, depth), ("x", "y", "c", "z"))
    ctx_axes = ("x", "y", "c")
    placed = (P(ctx_axes, "z"), P(ctx_axes, None), P(ctx_axes, "z"), P(ctx_axes, "z"), P())
    return jax.shard_map(
        functools.partial(shards, sides=sides, depth=depth),
        mesh=finer,
        in_specs=placed,
        out_specs=(P(ctx_axes, "z"), P(("x", "y", "c", "z"), None)),
        check_vma=False,
    )
```
